32 devices in a mesh: row: 8 (over z, x), col: 4 (over y, core).
Axes of the slice: x: 2, y: 2, z: 4, core: 2. Of those that a mesh axis runs over, the one named last changes fastest.
Arguments:
- p2_panel: bfloat16 [4096, 3584], P('row'), may hold values from -6 to 6
- density: bfloat16 [4096, 3584], P('row', 'col'), may hold values from -0.09375 to 0.09375
- pattern: int32 [64, 56], P('row'), may hold values 0 or 1
- x_basis: bfloat16 [4096, 32], P('row'), may hold values from -0.59765625 to 0.59765625
- x_offset: int32 [64], P('row'), may hold values from 0 to 160
- x_extent: int32 [64], P('row'), may hold values from 1 to 32
- y_basis: bfloat16 [8, 3584, 32], P('row', 'col'), may hold values from -0.59765625 to 0.59765625
- y_offset: int32 [8, 56], P('row', 'col'), may hold values from 0 to 160
- y_extent: int32 [8, 56], P('row', 'col'), may hold values from 1 to 32
Outputs:
- new_density: bfloat16 [4096, 3584], P('row', 'col')
- grid_density: float32 [1024, 512], P('row', 'col')
The draws below stay inside these ranges and needn't reach their ends.
Inputs may be any that keep to these rules, and one draw needn't show every extreme that they name: `pattern`: 1 where a block of the window is stored.
All inputs are finite; a program needn't handle non-finite values.
Results may differ from the reference program's by a relative error of at most 0.0049.
Values may be sent and summed in bfloat16 or wider, within the bound.
No kernel may reach another device: no remote copies, remote signals or barrier semaphores. Data moves between devices by JAX's collectives and lax.ppermute only.
A program may use at most 64 MiB of HBM per device.

```python
import jax
import jax.numpy as jnp
from jax import lax

BS = 64
BR = 8
HD = 3
SX = 128
SY = 128
TX = 32
TY = 32
M = 32
NB = 64
W = 56
WC = 14
NX = 1024
NY = 512
N_ROW = 8
N_COL = 4


def touch_ends(array, own_key, low, largest):
    spot = [jax.random.randint(jax.random.fold_in(own_key, axis), (), 0, length) for axis, length in enumerate(array.shape)]
    widest = array.shape.index(max(array.shape))
    beside = spot[:widest] + [(spot[widest] + 1) % array.shape[widest]] + spot[widest + 1:]
    return array.at[tuple(spot)].set(low).at[tuple(beside)].set(largest)


def block_scale(key, dims, cuts, smallest, top_value):
    level, own = 1.0, jax.random.fold_in(key, 6)
    for dim, parts in cuts:
        draws = jnp.exp(jax.random.uniform(jax.random.fold_in(own, dim), (parts,), jnp.float32, smallest / len(cuts), top_value / len(cuts)))
        level = level * jnp.repeat(draws, dims[dim] // parts).reshape([-1 if axis == dim else 1 for axis in range(len(dims))])
    return level


def normal_values(own_key, shape, scale, bound, shards=(), held_as=jnp.bfloat16):
    gain = block_scale(own_key, shape, shards, -0.22, 0.18) if shards else 1.0
    values = jax.random.normal(own_key, shape, jnp.float32) * scale * gain
    return jnp.minimum(jnp.maximum(values, -bound), bound).astype(held_as)


def setup_inputs(seed: int = 0) -> dict:
    splits = jax.random.split(jax.random.key(seed), 10)
    return {
        "p2_panel": normal_values(splits[0], (NB * BS, W * BS), 1.0, 6.0, ((0, 8),)),
        "density": normal_values(splits[1], (NB * BS, W * BS), (W * BS) ** -0.5, 0.09375, ((0, 8), (1, 4))),
        "pattern": touch_ends((jax.random.randint(splits[2], (NB, W), 0, 4) < 3).astype(jnp.int32), jax.random.fold_in(splits[2], 1), 0, 1),
        "x_basis": normal_values(splits[3], (NB * BS, TX), 0.1, 0.59765625, ((0, 8),)),
        "x_offset": touch_ends(jax.random.randint(splits[4], (NB,), 0, SX + 2 * M - TX + 1), jax.random.fold_in(splits[4], 1), 0, SX + 2 * M - TX).astype(jnp.int32),
        "x_extent": touch_ends(jax.random.randint(splits[5], (NB,), 1, TX + 1), jax.random.fold_in(splits[5], 1), 1, TX).astype(jnp.int32),
        "y_basis": normal_values(splits[6], (N_ROW, W * BS, TY), 0.1, 0.59765625, ((0, 8), (1, 4))),
        "y_offset": touch_ends(jax.random.randint(splits[7], (N_ROW, W), 0, SY + 2 * M - TY + 1), jax.random.fold_in(splits[7], 1), 0, SY + 2 * M - TY).astype(jnp.int32),
        "y_extent": touch_ends(jax.random.randint(splits[8], (N_ROW, W), 1, TY + 1), jax.random.fold_in(splits[8], 1), 1, TY).astype(jnp.int32),
    }


def mask_blocks(values, pattern):
    number, win_slots = pattern.shape
    block_size = values.shape[0] // number
    shaped = values.reshape(number, block_size, win_slots, block_size)
    return (shaped * pattern.astype(values.dtype)[:, None, :, None]).reshape(values.shape)


def place(tile_vals, offset, extent, length):
    number = offset.shape[0]
    breadth = tile_vals.shape[1]
    blocks = tile_vals.reshape(number, -1, breadth).astype(jnp.float32)
    cell_ids = jnp.arange(length, dtype=jnp.int32)
    step_ids = jnp.arange(breadth, dtype=jnp.int32)
    onehot = (cell_ids[None, None, :] == offset[:, None, None] + step_ids[None, :, None]) & (step_ids[None, :, None] < extent[:, None, None])
    spread = jnp.einsum("iat,ite->iae", blocks, onehot.astype(jnp.float32))
    return spread.reshape(-1, length).astype(jnp.bfloat16)


def natural_order(values):
    height = values.shape[0]
    return values.reshape(height, N_COL, WC, BS).transpose(0, 2, 1, 3).reshape(height, W * BS)


def class_order(values):
    height = values.shape[0]
    return values.reshape(height, WC, N_COL, BS).transpose(0, 2, 1, 3).reshape(height, W * BS)


def pick(values, index):
    return lax.dynamic_index_in_dim(values, index, 0, keepdims=False)


def reference(p2_panel, density, pattern, x_basis, x_offset, x_extent, y_basis, y_offset, y_extent):
    panel_rows = BR * BS
    square = mask_blocks(p2_panel, pattern).reshape(N_ROW, panel_rows, W * BS)
    stored = mask_blocks(natural_order(density), pattern).reshape(N_ROW, panel_rows, W * BS)
    patterns = pattern.reshape(N_ROW, BR, W)
    x_values = x_basis.reshape(N_ROW, panel_rows, TX)
    x_starts = x_offset.reshape(N_ROW, BR)
    x_sizes = x_extent.reshape(N_ROW, BR)

    def one_panel(panel):
        pieces = []
        for distance in range(-HD, HD + 1):
            source = pick(stored, (panel + distance) % N_ROW)
            cut_cols = BR * abs(distance) * BS
            if distance > 0:
                aligned = jnp.concatenate([jnp.zeros((panel_rows, cut_cols), source.dtype), source[:, : W * BS - cut_cols]], axis=1)
            elif distance < 0:
                aligned = jnp.concatenate([source[:, cut_cols:], jnp.zeros((panel_rows, cut_cols), source.dtype)], axis=1)
            else:
                aligned = source
            pieces.append(aligned)
        window = jnp.concatenate(pieces, axis=0)
        own_rows = pick(square, panel)
        product = jnp.dot(own_rows, window, preferred_element_type=jnp.float32)
        own_pattern = pick(patterns, panel)
        renewed = mask_blocks(3.0 * own_rows.astype(jnp.float32) - 2.0 * product, own_pattern).astype(jnp.bfloat16)
        renewed = class_order(renewed)
        y_spread = place(pick(y_basis, panel), pick(y_offset, panel), pick(y_extent, panel), SY + 2 * M)
        left_side = renewed.reshape(panel_rows, N_COL, WC * BS).astype(jnp.float32)
        right_side = y_spread.reshape(N_COL, WC * BS, SY + 2 * M).astype(jnp.float32)
        half_done = jnp.einsum("xcj,cjy->cxy", left_side, right_side).astype(jnp.bfloat16)
        x_spread = place(pick(x_values, panel), pick(x_starts, panel), pick(x_sizes, panel), SX + 2 * M)
        extended = jnp.einsum("xe,cxf->cef", x_spread.astype(jnp.float32), half_done.astype(jnp.float32))
        return renewed, extended

    renewed_all, extended = lax.map(one_panel, jnp.arange(N_ROW, dtype=jnp.int32))
    interior = extended[:, :, M:M + SX, :]
    interior = interior.at[:, :, SX - M:, :].add(jnp.roll(extended[:, :, :M, :], -1, axis=0))
    interior = interior.at[:, :, :M, :].add(jnp.roll(extended[:, :, SX + M:, :], 1, axis=0))
    grid_out = interior[:, :, :, M:M + SY]
    grid_out = grid_out.at[:, :, :, SY - M:].add(jnp.roll(interior[:, :, :, :M], -1, axis=1))
    grid_out = grid_out.at[:, :, :, :M].add(jnp.roll(interior[:, :, :, SY + M:], 1, axis=1))
    grid_density = grid_out.transpose(0, 2, 1, 3).reshape(NX, NY)
    return renewed_all.reshape(NB * BS, W * BS), grid_density
```

```python
import functools

import jax
import jax.numpy as jnp
from jax import lax
from jax.experimental import pallas as pl
from jax.experimental.pallas import tpu as pltpu
from jax.sharding import PartitionSpec as P

HD = 3
SX = 128
SY = 128
M = 32
EX = SX + 2 * M
EY = SY + 2 * M
CHUNKS = 2 * HD + 1
VMEM = pl.BlockSpec(memory_space=pltpu.VMEM)
SMEM = pl.BlockSpec(memory_space=pltpu.SMEM)
LIMIT = pltpu.CompilerParams(vmem_limit_bytes=40 * 1024 * 1024)
F32 = jnp.float32
BF16 = jnp.bfloat16


class Dims:
    def __init__(self, pattern, x_basis, n_col):
        self.br, self.win = pattern.shape
        self.bs = x_basis.shape[0] // self.br
        self.n_col = n_col
        self.wc = self.win // n_col
        self.stride = self.br // n_col
        self.uw = self.stride * self.bs
        self.rows = self.br * self.bs


def block_mask(pattern_ref, block_row, slots, bs, dtype):
    lane = lax.broadcasted_iota(jnp.int32, (1, bs * len(slots)), 1)
    row = jnp.zeros((1, bs * len(slots)), jnp.int32)
    for place, slot in enumerate(slots):
        inside = (lane >= place * bs) & (lane < (place + 1) * bs)
        row = jnp.where(inside, pattern_ref[block_row, slot], row)
    return row.astype(F32).astype(dtype)


def own_slots(dims, chunk, column):
    return [dims.n_col * (chunk * dims.stride + s) + column for s in range(dims.stride)]


def mask_kernel(dims, pattern_ref, density_ref, x1a_ref, x1b_ref, z1_ref):
    odd = lax.axis_index("row") % 2
    column = lax.axis_index("col")
    bs, uw = dims.bs, dims.uw
    near = x1a_ref.shape[0]
    for chunk in range(CHUNKS):
        for i in range(dims.br):
            rows = slice(i * bs, (i + 1) * bs)
            mask = block_mask(pattern_ref, i, own_slots(dims, chunk, column), bs, BF16)
            kept = density_ref[rows, chunk * uw : (chunk + 1) * uw] * mask
            for lane_odd in (0, 1):
                own = chunk if lane_odd else CHUNKS - 1 - chunk
                sent = CHUNKS - 1 - own

                @pl.when(odd == lane_odd)
                def _():
                    if sent < near:
                        x1a_ref[sent, rows, :] = kept
                    else:
                        x1b_ref[sent - near, rows, :] = kept
                    if own < near:
                        z1_ref[own, rows, :] = kept


def own_block_cols(dims, p2_ref, slot, column):
    pair = pl.multiple_of((dims.n_col * slot // 2 + column // 2) * 2 * dims.bs, 2 * dims.bs)
    wide = p2_ref[:, pl.ds(pair, 2 * dims.bs)].astype(F32)
    return jnp.where(column % 2 == 1, wide[:, dims.bs :], wide[:, : dims.bs])


def spread_kernel(
    dims,
    pattern_ref,
    x_offset_ref,
    x_extent_ref,
    y_offset_ref,
    y_extent_ref,
    p2_ref,
    x_basis_ref,
    y_basis_ref,
    squares_ref,
    summed_ref,
    xt_ref,
    y_ref,
):
    odd = lax.axis_index("row") % 2
    column = lax.axis_index("col")
    bs, uw, br = dims.bs, dims.uw, dims.br
    width = br * bs
    for block in range(CHUNKS):
        for i in range(br):
            rows = slice(i * bs, (i + 1) * bs)
            slots = [block * br + t for t in range(br)]
            mask = block_mask(pattern_ref, i, slots, bs, BF16)
            place = jnp.where(odd == 1, block, CHUNKS - 1 - block)
            squares_ref[place, rows, :] = p2_ref[rows, block * width : (block + 1) * width] * mask
    for chunk in range(CHUNKS):
        place = jnp.where(odd == 1, chunk, CHUNKS - 1 - chunk)
        parts = [
            own_block_cols(dims, p2_ref, chunk * dims.stride + s, column)
            for s in range(dims.stride)
        ]
        own = parts[0] if len(parts) == 1 else jnp.concatenate(parts, axis=1)
        summed_ref[place] = 1.5 * own
        for s in range(dims.stride):
            m = chunk * dims.stride + s
            tx = y_basis_ref.shape[1]
            step = lax.broadcasted_iota(jnp.int32, (tx, EY), 0)
            cell = lax.broadcasted_iota(jnp.int32, (tx, EY), 1)
            hit = (cell == y_offset_ref[0, m] + step) & (step < y_extent_ref[0, m])
            spread = jnp.dot(
                y_basis_ref[m * bs : (m + 1) * bs, :],
                hit.astype(F32).astype(BF16),
                preferred_element_type=F32,
            )
            y_ref[place, s * bs : (s + 1) * bs, :] = spread.astype(BF16)
    tx = x_basis_ref.shape[1]
    for i in range(br):
        step = lax.broadcasted_iota(jnp.int32, (EX, tx), 1)
        cell = lax.broadcasted_iota(jnp.int32, (EX, tx), 0)
        hit = (cell == x_offset_ref[i] + step) & (step < x_extent_ref[i])
        spread = lax.dot_general(
            hit.astype(F32).astype(BF16),
            x_basis_ref[i * bs : (i + 1) * bs, :],
            (((1,), (1,)), ((), ())),
            preferred_element_type=F32,
        )
        xt_ref[:, i * bs : (i + 1) * bs] = spread.astype(BF16)


def paired(terms):
    return [terms[at : at + 2] for at in range(0, len(terms), 2)]


def add_products(square, terms, summed_ref):
    for group in paired(terms):
        tiles = [tile[...] for _, tile in group]
        wide = tiles[0] if len(tiles) == 1 else jnp.concatenate(tiles, axis=1)
        product = jnp.dot(square, wide, preferred_element_type=F32)
        uw = tiles[0].shape[1]
        for at, (place, _) in enumerate(group):
            summed_ref[place] -= product[:, at * uw : (at + 1) * uw]


def first_kernel(squares_ref, before_ref, x1a_ref, x1b_ref, summed_ref):
    summed_ref[...] = before_ref[...]
    near = x1a_ref.shape[0]
    own = lambda j: x1a_ref.at[j] if j < near else x1b_ref.at[j - near]
    add_products(
        squares_ref[HD], [(k, own(CHUNKS - 1 - k)) for k in range(CHUNKS)], summed_ref
    )


def second_kernel(squares_ref, before_ref, x1a_ref, x1b_ref, z1_ref, summed_ref):
    summed_ref[...] = before_ref[...]
    near = x1a_ref.shape[0]
    partner = lambda j: x1a_ref.at[j] if j < near else x1b_ref.at[j - near]
    add_products(
        squares_ref[HD - 1], [(j - 1, partner(j)) for j in range(1, CHUNKS)], summed_ref
    )
    add_products(squares_ref[HD + 2], [(j + 2, z1_ref.at[j]) for j in range(5)], summed_ref)


def third_kernel(squares_ref, before_ref, z2a_ref, z2b_ref, x3_ref, summed_ref):
    summed_ref[...] = before_ref[...]
    next_tile = lambda j: z2a_ref.at[j] if j < 5 else z2b_ref.at[j - 5]
    add_products(
        squares_ref[HD + 1], [(j + 1, next_tile(j)) for j in range(6)], summed_ref
    )
    add_products(squares_ref[HD - 3], [(3 - j, x3_ref.at[j]) for j in range(4)], summed_ref)


def last_kernel(
    dims,
    pattern_ref,
    squares_ref,
    before_ref,
    x2_ref,
    z3_ref,
    xt_ref,
    y_ref,
    new_ref,
    middle_ref,
    rim_a_ref,
    rim_b_ref,
    summed_ref,
):
    odd = lax.axis_index("row") % 2
    column = lax.axis_index("col")
    bs, uw = dims.bs, dims.uw
    summed_ref[...] = before_ref[...]
    add_products(squares_ref[HD - 2], [(4 - j, x2_ref.at[j]) for j in range(5)], summed_ref)
    add_products(squares_ref[HD + 3], [(j + 3, z3_ref.at[j]) for j in range(4)], summed_ref)
    half = jnp.zeros((dims.rows, EY), F32)
    for k in range(CHUNKS):
        chunk = jnp.where(odd == 1, k, CHUNKS - 1 - k)
        pieces = []
        for i in range(dims.br):
            mask = block_mask(pattern_ref, i, own_slots(dims, chunk, column), bs, F32)
            pieces.append(summed_ref[k, i * bs : (i + 1) * bs, :] * (2.0 * mask))
        renewed = jnp.concatenate(pieces, axis=0).astype(BF16)
        for lane_odd in (0, 1):
            at = k if lane_odd else CHUNKS - 1 - k

            @pl.when(odd == lane_odd)
            def _():
                new_ref[:, at * uw : (at + 1) * uw] = renewed

        half = half + jnp.dot(renewed, y_ref[k], preferred_element_type=F32)
    extended = jnp.dot(xt_ref[...], half.astype(BF16), preferred_element_type=F32)
    middle_ref[...] = extended[M : M + SX]
    lower, upper = extended[:M], extended[SX + M :]
    rim_a_ref[...] = jnp.where(odd == 1, lower, upper)
    rim_b_ref[...] = jnp.where(odd == 1, upper, lower)


def row_rims_kernel(middle_ref, got_a_ref, got_b_ref, center_ref, rim_a_ref, rim_b_ref):
    odd = lax.axis_index("row") % 2
    col_odd = lax.axis_index("col") % 2
    got_a, got_b = got_a_ref[...], got_b_ref[...]
    low = jnp.where(odd == 1, got_a, got_b)
    high = jnp.where(odd == 1, got_b, got_a)
    interior = jnp.concatenate(
        [middle_ref[:M] + low, middle_ref[M : SX - M], middle_ref[SX - M :] + high], axis=0
    )
    center_ref[...] = interior[:, M : M + SY]
    lower, upper = interior[:, :M], interior[:, SY + M :]
    rim_a_ref[...] = jnp.where(col_odd == 1, lower, upper)
    rim_b_ref[...] = jnp.where(col_odd == 1, upper, lower)


def col_rims_kernel(center_ref, got_a_ref, got_b_ref, grid_ref):
    col_odd = lax.axis_index("col") % 2
    got_a, got_b = got_a_ref[...], got_b_ref[...]
    low = jnp.where(col_odd == 1, got_a, got_b)
    high = jnp.where(col_odd == 1, got_b, got_a)
    none = jnp.zeros((SX, SY - 2 * M), F32)
    grid_ref[...] = center_ref[...] + jnp.concatenate([low, none, high], axis=1)


def swap_partner(value, axis):
    count = lax.axis_size(axis)
    return lax.ppermute(value, axis, [(s, s ^ 1) for s in range(count)])


def swap_other(value, axis):
    count = lax.axis_size(axis)
    pairs = [(s, (s - 1) % count if s % 2 == 0 else (s + 1) % count) for s in range(count)]
    return lax.ppermute(value, axis, pairs)


def shift_level(value):
    count = lax.axis_size("row")
    pairs = [(s, (s + 2) % count if s % 2 == 0 else (s - 2) % count) for s in range(count)]
    return lax.ppermute(value, "row", pairs)


def after(value, *others):
    return lax.optimization_barrier((value,) + others)[0]


def call(kernel, outs, ins, scratch=(), flops=0):
    shapes = [jax.ShapeDtypeStruct(shape, dtype) for shape, dtype in outs]
    specs = [
        SMEM if jnp.issubdtype(value.dtype, jnp.integer) else VMEM for value in ins
    ]
    moved = sum(value.size * value.dtype.itemsize for value in list(ins) + shapes)
    return pl.pallas_call(
        kernel,
        out_shape=shapes,
        in_specs=specs,
        out_specs=[VMEM] * len(shapes),
        scratch_shapes=list(scratch),
        compiler_params=LIMIT,
        cost_estimate=pl.CostEstimate(flops=flops, bytes_accessed=moved, transcendentals=0),
    )(*ins)


def shards(p2_panel, density, pattern, x_basis, x_offset, x_extent, y_basis, y_offset, y_extent):
    dims = Dims(pattern, x_basis, lax.axis_size("col"))
    rows, uw = dims.rows, dims.uw
    per_chunk = 2 * rows * rows * uw
    chunks = lambda count: ((count, rows, uw), BF16)
    total = ((CHUNKS, rows, uw), F32)

    own_a, own_b, own_z = call(
        functools.partial(mask_kernel, dims), [chunks(5), chunks(2), chunks(5)], [pattern, density]
    )
    x1a = swap_partner(own_a, "row")
    z1 = shift_level(own_z)
    squares, summed, xt, y_spread = call(
        functools.partial(spread_kernel, dims),
        [((CHUNKS, rows, rows), BF16), total, ((EX, rows), BF16), ((CHUNKS, uw, EY), BF16)],
        [pattern, x_offset, x_extent, y_offset, y_extent, p2_panel, x_basis, y_basis[0]],
    )
    (summed,) = call(first_kernel, [total], [squares, summed, own_a, own_b], flops=7 * per_chunk)
    x1b = swap_partner(after(own_b, x1a), "row")
    z2a = shift_level(after(x1a, z1))
    x3 = swap_partner(after(z1[:4], x1b), "row")
    z2b = shift_level(after(x1b[:1], z1))
    (summed,) = call(
        second_kernel, [total], [squares, summed, x1a, x1b, z1], flops=11 * per_chunk
    )
    z3 = shift_level(after(z2a[:4], z2b))
    x2 = swap_partner(after(z2a, x3), "row")
    (summed,) = call(
        third_kernel, [total], [squares, summed, z2a, z2b, x3], flops=10 * per_chunk
    )
    new_density, middle, rim_a, rim_b = call(
        functools.partial(last_kernel, dims),
        [
            ((rows, dims.wc * dims.bs), BF16),
            ((SX, EY), F32),
            ((M, EY), F32),
            ((M, EY), F32),
        ],
        [pattern, squares, summed, x2, z3, xt, y_spread],
        scratch=[pltpu.VMEM((CHUNKS, rows, uw), F32)],
        flops=9 * per_chunk,
    )
    got_a = swap_partner(rim_a, "row")
    got_b = swap_other(rim_b, "row")
    center, rim_a, rim_b = call(
        row_rims_kernel,
        [((SX, SY), F32), ((SX, M), F32), ((SX, M), F32)],
        [middle, got_a, got_b],
    )
    got_a = swap_partner(rim_a, "col")
    got_b = swap_other(rim_b, "col")
    (grid_density,) = call(col_rims_kernel, [((SX, SY), F32)], [center, got_a, got_b])
    return new_density, grid_density


def solution(mesh):
    placed = (
        P("row", None),
        P("row", "col"),
        P("row", None),
        P("row", None),
        P("row"),
        P("row"),
        P("row", "col", None),
        P("row", "col"),
        P("row", "col"),
    )
    return jax.shard_map(
        shards,
        mesh=mesh,
        in_specs=placed,
        out_specs=(P("row", "col"), P("row", "col")),
        check_vma=False,
    )
```

```python
import functools

import jax
import jax.numpy as jnp
from jax import lax
from jax.experimental import pallas as pl
from jax.experimental.pallas import tpu as pltpu
from jax.sharding import PartitionSpec as P

HD = 3
SX = 128
SY = 128
M = 32
EX = SX + 2 * M
EY = SY + 2 * M
CHUNKS = 2 * HD + 1
VMEM = pl.BlockSpec(memory_space=pltpu.VMEM)
SMEM = pl.BlockSpec(memory_space=pltpu.SMEM)
F32 = jnp.float32
BF16 = jnp.bfloat16


class Dims:
    def __init__(self, pattern, x_basis, n_col):
        self.br, self.win = pattern.shape
        self.bs = x_basis.shape[0] // self.br
        self.n_col = n_col
        self.wc = self.win // n_col
        self.stride = self.br // n_col
        self.uw = self.stride * self.bs
        self.rows = self.br * self.bs


def block_mask(pattern_ref, block_row, slots, bs, dtype):
    lane = lax.broadcasted_iota(jnp.int32, (1, bs * len(slots)), 1)
    row = jnp.zeros((1, bs * len(slots)), jnp.int32)
    for place, slot in enumerate(slots):
        inside = (lane >= place * bs) & (lane < (place + 1) * bs)
        row = jnp.where(inside, pattern_ref[block_row, slot], row)
    return row.astype(F32).astype(dtype)


def own_slots(dims, chunk, column):
    return [dims.n_col * (chunk * dims.stride + s) + column for s in range(dims.stride)]


def mask_kernel(
    dims, pattern_hbm, density_hbm, x1a_ref, x1b_ref, z1_ref, pattern_ref, tile_ref, pattern_sem, sems
):
    odd = lax.axis_index("row") % 2
    column = lax.axis_index("col")
    bs, uw = dims.bs, dims.uw
    near = x1a_ref.shape[0]
    wide = tile_ref.shape[2]
    fetch_pattern = pltpu.make_async_copy(pattern_hbm, pattern_ref, pattern_sem)
    fetch_pattern.start()
    parts = tile_ref.shape[0]
    fetches = []
    for part in range(parts):
        cols = pl.ds(part * wide, wide)
        fetch = pltpu.make_async_copy(density_hbm.at[:, cols], tile_ref.at[part], sems.at[part])
        fetch.start()
        fetches.append(fetch)
    fetch_pattern.wait()
    arrived = 0
    for chunk in range(CHUNKS):
        part, start = divmod(chunk * uw, wide)
        if part == arrived:
            fetches[part].wait()
            arrived += 1
        for i in range(dims.br):
            rows = slice(i * bs, (i + 1) * bs)
            mask = block_mask(pattern_ref, i, own_slots(dims, chunk, column), bs, BF16)
            kept = tile_ref[part, rows, start : start + uw] * mask
            for lane_odd in (0, 1):
                own = chunk if lane_odd else CHUNKS - 1 - chunk
                sent = CHUNKS - 1 - own

                @pl.when(odd == lane_odd)
                def _():
                    if sent < near:
                        x1a_ref[sent, rows, :] = kept
                    else:
                        x1b_ref[sent - near, rows, :] = kept
                    if own < near:
                        z1_ref[own, rows, :] = kept


def own_block_cols(dims, p2_ref, slot, column):
    pair = pl.multiple_of((dims.n_col * slot // 2 + column // 2) * 2 * dims.bs, 2 * dims.bs)
    wide = p2_ref[:, pl.ds(pair, 2 * dims.bs)].astype(F32)
    return jnp.where(column % 2 == 1, wide[:, dims.bs :], wide[:, : dims.bs])


def spread_kernel(
    dims,
    pattern_ref,
    x_offset_ref,
    x_extent_ref,
    y_offset_ref,
    y_extent_ref,
    p2_ref,
    x_basis_ref,
    y_basis_ref,
    squares_ref,
    summed_ref,
    xt_ref,
    y_ref,
    mask_ref,
):
    odd = lax.axis_index("row") % 2
    column = lax.axis_index("col")
    bs, uw, br = dims.bs, dims.uw, dims.br
    width = br * bs
    for block in range(CHUNKS):
        for i in range(br):
            rows = slice(i * bs, (i + 1) * bs)
            slots = [block * br + t for t in range(br)]
            mask = block_mask(pattern_ref, i, slots, bs, BF16)
            place = jnp.where(odd == 1, block, CHUNKS - 1 - block)
            squares_ref[place, rows, :] = p2_ref[rows, block * width : (block + 1) * width] * mask
    for chunk in range(CHUNKS):
        place = jnp.where(odd == 1, chunk, CHUNKS - 1 - chunk)
        parts = [
            own_block_cols(dims, p2_ref, chunk * dims.stride + s, column)
            for s in range(dims.stride)
        ]
        own = parts[0] if len(parts) == 1 else jnp.concatenate(parts, axis=1)
        summed_ref[place] = 1.5 * own
        for i in range(br):
            slots = own_slots(dims, chunk, column)
            mask_ref[place, i : i + 1, :] = 2.0 * block_mask(pattern_ref, i, slots, bs, F32)
        for s in range(dims.stride):
            m = chunk * dims.stride + s
            tx = y_basis_ref.shape[1]
            step = lax.broadcasted_iota(jnp.int32, (tx, EY), 0)
            cell = lax.broadcasted_iota(jnp.int32, (tx, EY), 1)
            hit = (cell == y_offset_ref[0, m] + step) & (step < y_extent_ref[0, m])
            spread = jnp.dot(
                y_basis_ref[m * bs : (m + 1) * bs, :],
                hit.astype(F32).astype(BF16),
                preferred_element_type=F32,
            )
            y_ref[place, s * bs : (s + 1) * bs, :] = spread.astype(BF16)
    tx = x_basis_ref.shape[1]
    for i in range(br):
        step = lax.broadcasted_iota(jnp.int32, (EX, tx), 1)
        cell = lax.broadcasted_iota(jnp.int32, (EX, tx), 0)
        hit = (cell == x_offset_ref[i] + step) & (step < x_extent_ref[i])
        spread = lax.dot_general(
            hit.astype(F32).astype(BF16),
            x_basis_ref[i * bs : (i + 1) * bs, :],
            (((1,), (1,)), ((), ())),
            preferred_element_type=F32,
        )
        xt_ref[:, i * bs : (i + 1) * bs] = spread.astype(BF16)


def paired(terms):
    return [terms[at : at + 2] for at in range(0, len(terms), 2)]


def add_products(square, terms, summed_ref):
    for group in paired(terms):
        tiles = [tile[...] for _, tile in group]
        wide = tiles[0] if len(tiles) == 1 else jnp.concatenate(tiles, axis=1)
        product = jnp.dot(square, wide, preferred_element_type=F32)
        uw = tiles[0].shape[1]
        for at, (place, _) in enumerate(group):
            summed_ref[place] -= product[:, at * uw : (at + 1) * uw]


def first_kernel(squares_ref, before_ref, x1a_ref, x1b_ref, summed_ref):
    summed_ref[...] = before_ref[...]
    near = x1a_ref.shape[0]
    own = lambda j: x1a_ref.at[j] if j < near else x1b_ref.at[j - near]
    add_products(
        squares_ref[HD], [(k, own(CHUNKS - 1 - k)) for k in range(CHUNKS)], summed_ref
    )


def second_kernel(squares_ref, before_ref, x1a_ref, z1_ref, summed_ref):
    summed_ref[...] = before_ref[...]
    add_products(squares_ref[HD - 1], [(j - 1, x1a_ref.at[j]) for j in range(1, 5)], summed_ref)
    add_products(squares_ref[HD + 2], [(j + 2, z1_ref.at[j]) for j in range(5)], summed_ref)


def third_kernel(squares_ref, before_ref, z2a_ref, x1b_ref, x3_ref, summed_ref):
    summed_ref[...] = before_ref[...]
    add_products(squares_ref[HD + 1], [(j + 1, z2a_ref.at[j]) for j in range(5)], summed_ref)
    add_products(squares_ref[HD - 1], [(4 + j, x1b_ref.at[j]) for j in range(2)], summed_ref)
    add_products(squares_ref[HD - 3], [(3 - j, x3_ref.at[j]) for j in range(4)], summed_ref)


def fourth_kernel(squares_ref, before_ref, z2b_ref, z3_ref, summed_ref):
    summed_ref[...] = before_ref[...]
    add_products(squares_ref[HD + 1], [(6, z2b_ref.at[0])], summed_ref)
    add_products(squares_ref[HD + 3], [(j + 3, z3_ref.at[j]) for j in range(4)], summed_ref)


def last_kernel(
    dims,
    mask_ref,
    squares_ref,
    before_ref,
    x2_ref,
    xt_ref,
    y_ref,
    new_ref,
    middle_ref,
    rim_a_ref,
    rim_b_ref,
):
    odd = lax.axis_index("row") % 2
    bs, uw = dims.bs, dims.uw

    def finish(k, total):
        for i in range(dims.br):
            rows = slice(i * bs, (i + 1) * bs)
            kept = total[rows] * mask_ref[k, i : i + 1, :]
            new_ref[rows, k * uw : (k + 1) * uw] = kept.astype(BF16)

    for group in ((0, 1), (2, 3), (4,)):
        tiles = [x2_ref[4 - k] for k in group]
        wide = tiles[0] if len(tiles) == 1 else jnp.concatenate(tiles, axis=1)
        product = jnp.dot(squares_ref[HD - 2], wide, preferred_element_type=F32)
        for at, k in enumerate(group):
            finish(k, before_ref[k] - product[:, at * uw : (at + 1) * uw])
    for k in (5, 6):
        finish(k, before_ref[k])
    half = jnp.dot(
        new_ref[...], y_ref[...].reshape(CHUNKS * uw, EY), preferred_element_type=F32
    )
    extended = jnp.dot(xt_ref[...], half.astype(BF16), preferred_element_type=F32)
    middle_ref[...] = extended[M : M + SX]
    lower, upper = extended[:M], extended[SX + M :]
    rim_a_ref[...] = jnp.where(odd == 1, lower, upper)
    rim_b_ref[...] = jnp.where(odd == 1, upper, lower)


def order_kernel(dims, own_ref, new_ref):
    odd = lax.axis_index("row") % 2
    uw = dims.uw

    @pl.when(odd == 1)
    def _():
        new_ref[...] = own_ref[...]

    @pl.when(odd == 0)
    def _():
        for k in range(CHUNKS):
            at = CHUNKS - 1 - k
            new_ref[:, at * uw : (at + 1) * uw] = own_ref[:, k * uw : (k + 1) * uw]


def row_rims_kernel(middle_ref, got_a_ref, got_b_ref, center_ref, rim_a_ref, rim_b_ref):
    odd = lax.axis_index("row") % 2
    col_odd = lax.axis_index("col") % 2
    got_a, got_b = got_a_ref[...], got_b_ref[...]
    low = jnp.where(odd == 1, got_a, got_b)
    high = jnp.where(odd == 1, got_b, got_a)
    interior = jnp.concatenate(
        [middle_ref[:M] + low, middle_ref[M : SX - M], middle_ref[SX - M :] + high], axis=0
    )
    center_ref[...] = interior[:, M : M + SY]
    lower, upper = interior[:, :M], interior[:, SY + M :]
    rim_a_ref[...] = jnp.where(col_odd == 1, lower, upper)
    rim_b_ref[...] = jnp.where(col_odd == 1, upper, lower)


def col_rims_kernel(center_ref, got_a_ref, got_b_ref, grid_ref):
    col_odd = lax.axis_index("col") % 2
    got_a, got_b = got_a_ref[...], got_b_ref[...]
    low = jnp.where(col_odd == 1, got_a, got_b)
    high = jnp.where(col_odd == 1, got_b, got_a)
    none = jnp.zeros((SX, SY - 2 * M), F32)
    grid_ref[...] = center_ref[...] + jnp.concatenate([low, none, high], axis=1)


def swap_partner(value, axis):
    count = lax.axis_size(axis)
    return lax.ppermute(value, axis, [(s, s ^ 1) for s in range(count)])


def swap_other(value, axis):
    count = lax.axis_size(axis)
    pairs = [(s, (s - 1) % count if s % 2 == 0 else (s + 1) % count) for s in range(count)]
    return lax.ppermute(value, axis, pairs)


def shift_level(value):
    count = lax.axis_size("row")
    pairs = [(s, (s + 2) % count if s % 2 == 0 else (s - 2) % count) for s in range(count)]
    return lax.ppermute(value, "row", pairs)


def after(value, *others):
    return lax.optimization_barrier((value,) + others)[0]


def call(kernel, outs, ins, scratch=(), beside=0, stay=(), limit=24):
    shapes = [jax.ShapeDtypeStruct(shape, dtype) for shape, dtype in outs]
    specs = [
        pl.BlockSpec(memory_space=pltpu.HBM)
        if at in stay
        else SMEM
        if jnp.issubdtype(value.dtype, jnp.integer)
        else VMEM
        for at, value in enumerate(ins)
    ]
    moved = sum(value.size * value.dtype.itemsize for value in list(ins) + shapes)
    return pl.pallas_call(
        kernel,
        out_shape=shapes,
        in_specs=specs,
        out_specs=[VMEM] * len(shapes),
        scratch_shapes=list(scratch),
        compiler_params=pltpu.CompilerParams(vmem_limit_bytes=limit * 2**20),
        cost_estimate=pl.CostEstimate(
            flops=beside * 10**9, bytes_accessed=moved, transcendentals=0
        ),
    )(*ins)


def shards(p2_panel, density, pattern, x_basis, x_offset, x_extent, y_basis, y_offset, y_extent):
    dims = Dims(pattern, x_basis, lax.axis_size("col"))
    rows, uw = dims.rows, dims.uw
    chunks = lambda count: ((count, rows, uw), BF16)
    total = ((CHUNKS, rows, uw), F32)

    parts = CHUNKS if uw % 128 == 0 else 1
    own_a, own_b, own_z = call(
        functools.partial(mask_kernel, dims),
        [chunks(5), chunks(2), chunks(5)],
        [pattern, density],
        scratch=[
            pltpu.SMEM(pattern.shape, jnp.int32),
            pltpu.VMEM((parts, rows, CHUNKS * uw // parts), BF16),
            pltpu.SemaphoreType.DMA(()),
            pltpu.SemaphoreType.DMA((parts,)),
        ],
        stay=(0, 1),
        limit=60,
    )
    x1a = swap_partner(own_a, "row")
    z1 = shift_level(own_z)
    squares, summed, xt, y_spread, mask = call(
        functools.partial(spread_kernel, dims),
        [
            ((CHUNKS, rows, rows), BF16),
            total,
            ((EX, rows), BF16),
            ((CHUNKS, uw, EY), BF16),
            ((CHUNKS, dims.br, uw), F32),
        ],
        [pattern, x_offset, x_extent, y_offset, y_extent, p2_panel, x_basis, y_basis[0]],
        beside=12,
    )
    (summed,) = call(first_kernel, [total], [squares, summed, own_a, own_b])
    z2a = shift_level(after(x1a, summed))
    x1b = swap_partner(after(own_b, x1a, summed), "row")
    x3 = swap_partner(z1[:4], "row")
    (summed,) = call(second_kernel, [total], [squares, summed, x1a, z1], beside=12)
    x2 = swap_partner(z2a, "row")
    z3 = shift_level(z2a[:4])
    z2b = shift_level(after(x1b[:1], z2a))
    (summed,) = call(third_kernel, [total], [squares, summed, z2a, x1b, x3], beside=12)
    (summed,) = call(fourth_kernel, [total], [squares, summed, z2b, z3])
    new_own, middle, rim_a, rim_b = call(
        functools.partial(last_kernel, dims),
        [
            ((rows, dims.wc * dims.bs), BF16),
            ((SX, EY), F32),
            ((M, EY), F32),
            ((M, EY), F32),
        ],
        [mask, squares, summed, x2, xt, y_spread],
    )
    (new_density,) = call(
        functools.partial(order_kernel, dims), [(new_own.shape, BF16)], [new_own]
    )
    got_a = swap_partner(rim_a, "row")
    got_b = swap_other(rim_b, "row")
    center, rim_a, rim_b = call(
        row_rims_kernel,
        [((SX, SY), F32), ((SX, M), F32), ((SX, M), F32)],
        [middle, got_a, got_b],
    )
    got_a = swap_partner(rim_a, "col")
    got_b = swap_other(rim_b, "col")
    (grid_density,) = call(col_rims_kernel, [((SX, SY), F32)], [center, got_a, got_b])
    return new_density, grid_density


def solution(mesh):
    placed = (
        P("row", None),
        P("row", "col"),
        P("row", None),
        P("row", None),
        P("row"),
        P("row"),
        P("row", "col", None),
        P("row", "col"),
        P("row", "col"),
    )
    return jax.shard_map(
        shards,
        mesh=mesh,
        in_specs=placed,
        out_specs=(P("row", "col"), P("row", "col")),
        check_vma=False,
    )
```

```python
import functools

import jax
import jax.numpy as jnp
from jax import lax
from jax.experimental import pallas as pl
from jax.experimental.pallas import tpu as pltpu
from jax.sharding import PartitionSpec as P

HD = 3
SX = 128
SY = 128
M = 32
EX = SX + 2 * M
EY = SY + 2 * M
CHUNKS = 2 * HD + 1
NEAR = 4
KA, K1, KE, KB, KC = 12, 4, 1, 0, 5
D_Z2P, D_X1Q, D_X3, D_X2Q, D_Z2Q, D_X2P, D_KE, D_ZB, D_ORD, D_Z1 = 1, 0, 1, 0, 0, 1, 0, 1, 1, 0
VMEM = pl.BlockSpec(memory_space=pltpu.VMEM)
SMEM = pl.BlockSpec(memory_space=pltpu.SMEM)
F32 = jnp.float32
BF16 = jnp.bfloat16


class Dims:
    def __init__(self, pattern, x_basis, n_col):
        self.br, self.win = pattern.shape
        self.bs = x_basis.shape[0] // self.br
        self.n_col = n_col
        self.wc = self.win // n_col
        self.stride = self.br // n_col
        self.uw = self.stride * self.bs
        self.rows = self.br * self.bs


def block_mask(pattern_ref, block_row, slots, bs, dtype):
    lane = lax.broadcasted_iota(jnp.int32, (1, bs * len(slots)), 1)
    row = jnp.zeros((1, bs * len(slots)), jnp.int32)
    for place, slot in enumerate(slots):
        inside = (lane >= place * bs) & (lane < (place + 1) * bs)
        row = jnp.where(inside, pattern_ref[block_row, slot], row)
    return row.astype(F32).astype(dtype)


def own_slots(dims, chunk, column):
    return [dims.n_col * (chunk * dims.stride + s) + column for s in range(dims.stride)]


def mask_kernel(
    dims,
    pattern_hbm,
    density_hbm,
    x1a_ref,
    x1b_ref,
    *refs,
):
    z1_refs, refs = refs[:-8], refs[-8:]
    pattern_ref, tile_ref, kept_ref, pattern_sem, tile_sems, x1a_sem, x1b_sem, z1_sem = refs
    odd = lax.axis_index("row") % 2
    column = lax.axis_index("col")
    bs, uw = dims.bs, dims.uw
    wide = tile_ref.shape[2]
    fetch_pattern = pltpu.make_async_copy(pattern_hbm, pattern_ref, pattern_sem)
    fetch_pattern.start()
    fetches = []
    for part in range(tile_ref.shape[0]):
        cols = pl.ds(part * wide, wide)
        fetch = pltpu.make_async_copy(density_hbm.at[:, cols], tile_ref.at[part], tile_sems.at[part])
        fetch.start()
        fetches.append(fetch)
    fetch_pattern.wait()
    arrived = 0
    for chunk in range(CHUNKS):
        part, start = divmod(chunk * uw, wide)
        if part == arrived:
            fetches[part].wait()
            arrived += 1
        for i in range(dims.br):
            rows = slice(i * bs, (i + 1) * bs)
            mask = block_mask(pattern_ref, i, own_slots(dims, chunk, column), bs, BF16)
            kept_ref[chunk, rows, :] = tile_ref[part, rows, start : start + uw] * mask
    own = lambda k: jnp.where(odd == 1, k, CHUNKS - 1 - k)
    copies = []
    for j in range(CHUNKS):
        near = x1a_ref.shape[0]
        dest, sem = (x1a_ref.at[j], x1a_sem.at[j]) if j < near else (x1b_ref.at[j - near], x1b_sem.at[j - near])
        copies.append(pltpu.make_async_copy(kept_ref.at[own(CHUNKS - 1 - j)], dest, sem))
        copies[-1].start()
    first = z1_refs[0].shape[0]
    for k in range(5):
        dest = z1_refs[0].at[k] if k < first else z1_refs[1].at[k - first]
        copies.append(pltpu.make_async_copy(kept_ref.at[own(k)], dest, z1_sem.at[k]))
        copies[-1].start()
    for copy in copies:
        copy.wait()


def own_block_cols(dims, p2_ref, slot, column):
    pair = pl.multiple_of((dims.n_col * slot // 2 + column // 2) * 2 * dims.bs, 2 * dims.bs)
    wide = p2_ref[:, pl.ds(pair, 2 * dims.bs)].astype(F32)
    return jnp.where(column % 2 == 1, wide[:, dims.bs :], wide[:, : dims.bs])


def spread_kernel(
    dims,
    pattern_ref,
    x_offset_ref,
    x_extent_ref,
    y_offset_ref,
    y_extent_ref,
    p2_ref,
    x_basis_ref,
    y_basis_ref,
    squares_ref,
    summed_ref,
    xt_ref,
    y_ref,
    mask_ref,
):
    odd = lax.axis_index("row") % 2
    column = lax.axis_index("col")
    bs, uw, br = dims.bs, dims.uw, dims.br
    width = br * bs
    for block in range(CHUNKS):
        for i in range(br):
            rows = slice(i * bs, (i + 1) * bs)
            slots = [block * br + t for t in range(br)]
            mask = block_mask(pattern_ref, i, slots, bs, BF16)
            place = jnp.where(odd == 1, block, CHUNKS - 1 - block)
            squares_ref[place, rows, :] = p2_ref[rows, block * width : (block + 1) * width] * mask
    for chunk in range(CHUNKS):
        place = jnp.where(odd == 1, chunk, CHUNKS - 1 - chunk)
        parts = [
            own_block_cols(dims, p2_ref, chunk * dims.stride + s, column)
            for s in range(dims.stride)
        ]
        own = parts[0] if len(parts) == 1 else jnp.concatenate(parts, axis=1)
        summed_ref[place] = 1.5 * own
        for i in range(br):
            slots = own_slots(dims, chunk, column)
            mask_ref[place, i : i + 1, :] = 2.0 * block_mask(pattern_ref, i, slots, bs, F32)
        for s in range(dims.stride):
            m = chunk * dims.stride + s
            tx = y_basis_ref.shape[1]
            step = lax.broadcasted_iota(jnp.int32, (tx, EY), 0)
            cell = lax.broadcasted_iota(jnp.int32, (tx, EY), 1)
            hit = (cell == y_offset_ref[0, m] + step) & (step < y_extent_ref[0, m])
            spread = jnp.dot(
                y_basis_ref[m * bs : (m + 1) * bs, :],
                hit.astype(F32).astype(BF16),
                preferred_element_type=F32,
            )
            y_ref[place, s * bs : (s + 1) * bs, :] = spread.astype(BF16)
    tx = x_basis_ref.shape[1]
    for i in range(br):
        step = lax.broadcasted_iota(jnp.int32, (EX, tx), 1)
        cell = lax.broadcasted_iota(jnp.int32, (EX, tx), 0)
        hit = (cell == x_offset_ref[i] + step) & (step < x_extent_ref[i])
        spread = lax.dot_general(
            hit.astype(F32).astype(BF16),
            x_basis_ref[i * bs : (i + 1) * bs, :],
            (((1,), (1,)), ((), ())),
            preferred_element_type=F32,
        )
        xt_ref[:, i * bs : (i + 1) * bs] = spread.astype(BF16)


def paired(terms):
    return [terms[at : at + 2] for at in range(0, len(terms), 2)]


def add_products(square, terms, summed_ref):
    for group in paired(terms):
        tiles = [tile[...] for _, tile in group]
        wide = tiles[0] if len(tiles) == 1 else jnp.concatenate(tiles, axis=1)
        product = jnp.dot(square, wide, preferred_element_type=F32)
        uw = tiles[0].shape[1]
        for at, (place, _) in enumerate(group):
            summed_ref[place] -= product[:, at * uw : (at + 1) * uw]


def first_kernel(squares_ref, before_ref, x1a_ref, x1b_ref, summed_ref):
    summed_ref[...] = before_ref[...]
    near = x1a_ref.shape[0]
    own = lambda j: x1a_ref.at[j] if j < near else x1b_ref.at[j - near]
    add_products(
        squares_ref[HD], [(k, own(CHUNKS - 1 - k)) for k in range(CHUNKS)], summed_ref
    )


def stage_kernel(counts, terms, squares_ref, before_ref, *refs):
    summed_ref = refs[-1]
    summed_ref[...] = before_ref[...]
    for distance, pairs in terms:
        add_products(
            squares_ref[HD + distance],
            [(place, refs[which].at[at]) for place, which, at in pairs],
            summed_ref,
        )


def last_kernel(
    dims,
    mask_ref,
    squares_ref,
    before_ref,
    *refs,
):
    xt_ref, y_ref, new_ref, middle_ref, rim_a_ref, rim_b_ref = refs[-6:]
    x2_refs = refs[:-6]
    odd = lax.axis_index("row") % 2
    bs, uw = dims.bs, dims.uw

    x2_tile = lambda j: x2_refs[0][j] if j < NEAR else x2_refs[1][j - NEAR]

    def finish(k, total):
        for i in range(dims.br):
            rows = slice(i * bs, (i + 1) * bs)
            kept = total[rows] * mask_ref[k, i : i + 1, :]
            new_ref[rows, k * uw : (k + 1) * uw] = kept.astype(BF16)

    for group in ((0, 1), (2, 3), (4,)):
        tiles = [x2_tile(4 - k) for k in group]
        wide = tiles[0] if len(tiles) == 1 else jnp.concatenate(tiles, axis=1)
        product = jnp.dot(squares_ref[HD - 2], wide, preferred_element_type=F32)
        for at, k in enumerate(group):
            finish(k, before_ref[k] - product[:, at * uw : (at + 1) * uw])
    for k in (5, 6):
        finish(k, before_ref[k])
    half = jnp.dot(
        new_ref[...], y_ref[...].reshape(CHUNKS * uw, EY), preferred_element_type=F32
    )
    extended = jnp.dot(xt_ref[...], half.astype(BF16), preferred_element_type=F32)
    middle_ref[...] = extended[M : M + SX]
    lower, upper = extended[:M], extended[SX + M :]
    rim_a_ref[...] = jnp.where(odd == 1, lower, upper)
    rim_b_ref[...] = jnp.where(odd == 1, upper, lower)


def order_kernel(dims, own_ref, new_ref):
    odd = lax.axis_index("row") % 2
    uw = dims.uw

    @pl.when(odd == 1)
    def _():
        new_ref[...] = own_ref[...]

    @pl.when(odd == 0)
    def _():
        for k in range(CHUNKS):
            at = CHUNKS - 1 - k
            new_ref[:, at * uw : (at + 1) * uw] = own_ref[:, k * uw : (k + 1) * uw]


def row_rims_kernel(middle_ref, got_a_ref, got_b_ref, center_ref, rim_a_ref, rim_b_ref):
    odd = lax.axis_index("row") % 2
    col_odd = lax.axis_index("col") % 2
    got_a, got_b = got_a_ref[...], got_b_ref[...]
    low = jnp.where(odd == 1, got_a, got_b)
    high = jnp.where(odd == 1, got_b, got_a)
    interior = jnp.concatenate(
        [middle_ref[:M] + low, middle_ref[M : SX - M], middle_ref[SX - M :] + high], axis=0
    )
    center_ref[...] = interior[:, M : M + SY]
    lower, upper = interior[:, :M], interior[:, SY + M :]
    rim_a_ref[...] = jnp.where(col_odd == 1, lower, upper)
    rim_b_ref[...] = jnp.where(col_odd == 1, upper, lower)


def col_rims_kernel(center_ref, got_a_ref, got_b_ref, grid_ref):
    col_odd = lax.axis_index("col") % 2
    got_a, got_b = got_a_ref[...], got_b_ref[...]
    low = jnp.where(col_odd == 1, got_a, got_b)
    high = jnp.where(col_odd == 1, got_b, got_a)
    none = jnp.zeros((SX, SY - 2 * M), F32)
    grid_ref[...] = center_ref[...] + jnp.concatenate([low, none, high], axis=1)


def swap_partner(value, axis):
    count = lax.axis_size(axis)
    return lax.ppermute(value, axis, [(s, s ^ 1) for s in range(count)])


def swap_other(value, axis):
    count = lax.axis_size(axis)
    pairs = [(s, (s - 1) % count if s % 2 == 0 else (s + 1) % count) for s in range(count)]
    return lax.ppermute(value, axis, pairs)


def shift_level(value):
    count = lax.axis_size("row")
    pairs = [(s, (s + 2) % count if s % 2 == 0 else (s - 2) % count) for s in range(count)]
    return lax.ppermute(value, "row", pairs)


def after(value, *others):
    return lax.optimization_barrier((value,) + others)[0]


def call(kernel, outs, ins, scratch=(), beside=0, stay=(), limit=24, out_stay=False, light=False):
    shapes = [jax.ShapeDtypeStruct(shape, dtype) for shape, dtype in outs]
    specs = [
        pl.BlockSpec(memory_space=pltpu.HBM)
        if at in stay
        else SMEM
        if jnp.issubdtype(value.dtype, jnp.integer)
        else VMEM
        for at, value in enumerate(ins)
    ]
    moved = sum(value.size * value.dtype.itemsize for value in list(ins) + shapes)
    return pl.pallas_call(
        kernel,
        out_shape=shapes,
        in_specs=specs,
        out_specs=[pl.BlockSpec(memory_space=pltpu.HBM if out_stay else VMEM.memory_space)] * len(shapes),
        scratch_shapes=list(scratch),
        compiler_params=pltpu.CompilerParams(vmem_limit_bytes=limit * 2**20),
        cost_estimate=pl.CostEstimate(
            flops=beside * 10**9, bytes_accessed=0 if light else moved, transcendentals=0
        ),
    )(*ins)


def shards(p2_panel, density, pattern, x_basis, x_offset, x_extent, y_basis, y_offset, y_extent):
    dims = Dims(pattern, x_basis, lax.axis_size("col"))
    rows, uw = dims.rows, dims.uw
    chunks = lambda count: ((count, rows, uw), BF16)
    total = ((CHUNKS, rows, uw), F32)

    parts = CHUNKS if uw % 128 == 0 else 1
    own_a, own_b, *own_z = call(
        functools.partial(mask_kernel, dims),
        [chunks(NEAR), chunks(CHUNKS - NEAR)] + ([chunks(4), chunks(1)] if D_ZB else [chunks(5)]),
        [pattern, density],
        scratch=[
            pltpu.SMEM(pattern.shape, jnp.int32),
            pltpu.VMEM((parts, rows, CHUNKS * uw // parts), BF16),
            pltpu.VMEM((CHUNKS, rows, uw), BF16),
            pltpu.SemaphoreType.DMA(()),
            pltpu.SemaphoreType.DMA((parts,)),
            pltpu.SemaphoreType.DMA((NEAR,)),
            pltpu.SemaphoreType.DMA((CHUNKS - NEAR,)),
            pltpu.SemaphoreType.DMA((5,)),
        ],
        stay=(0, 1),
        limit=60,
        out_stay=True,
    )
    if D_ORD == 0:
        x1p = swap_partner(own_a, "row")
        z1 = shift_level(own_z[0])
        x1q = swap_partner(own_b, "row") if D_X1Q == 0 else None
    else:
        x1q = swap_partner(own_b, "row") if D_X1Q == 0 else None
        z1 = shift_level(own_z[0])
        x1p = swap_partner(own_a, "row")
    squares, summed, xt, y_spread, mask = call(
        functools.partial(spread_kernel, dims),
        [
            ((CHUNKS, rows, rows), BF16),
            total,
            ((EX, rows), BF16),
            ((CHUNKS, uw, EY), BF16),
            ((CHUNKS, dims.br, uw), F32),
        ],
        [pattern, x_offset, x_extent, y_offset, y_extent, p2_panel, x_basis, y_basis[0]],
        beside=KA,
    )
    if D_X1Q == 1:
        x1q = swap_partner(after(own_b, summed), "row")
    (summed,) = call(first_kernel, [total], [squares, summed, own_a, own_b], beside=K1)
    if D_X1Q == 2:
        x1q = swap_partner(after(own_b, x1p), "row")
    z2p = shift_level(after(x1p, *([[], [summed], [z1], [summed, z1]][D_Z2P])))
    x3 = swap_partner(after(z1[:4], *([[], [x1p], [summed]][D_X3])), "row")
    z2q = shift_level(after(x1q[: 6 - NEAR], *([[], [z1], [summed], [z1, summed]][D_Z2Q])))
    z1b = shift_level(own_z[1]) if D_ZB else None

    def stage(summed, beside, ins, terms):
        which = {id(value): at for at, value in enumerate(ins)}
        listed = [
            (distance, [(place, which[id(value)], at) for place, value, at in pairs])
            for distance, pairs in terms
        ]
        return call(
            functools.partial(stage_kernel, None, listed),
            [total],
            [squares, summed] + ins,
            beside=beside,
        )[0]

    near_terms = [(j - 1, x1p, j) for j in range(1, NEAR)]
    rest_terms = [(j - 1, x1q, j - NEAR) for j in range(NEAR, CHUNKS)]
    z1_terms = [(j + 2, z1, j) for j in range(4)]
    z1_rest = (6, z1b, 0) if D_ZB else (6, z1, 4)
    if D_KE:
        summed = stage(summed, KE, [x1p, x1q, z1], [(-1, near_terms + rest_terms), (2, z1_terms)])
    else:
        summed = stage(summed, KE, [x1p, z1], [(-1, near_terms), (2, z1_terms)])
    x2p = swap_partner(after(z2p, *([[], [x3], [summed]][D_X2P])), "row")
    z3 = shift_level(z2p[:4])
    summed = stage(summed, KB, [z2p], [(1, [(j + 1, z2p, j) for j in range(NEAR)])])
    x2 = [x2p]
    if NEAR < 5:
        x2.append(
            swap_partner(after(z2q[: 5 - NEAR], *([[], [x3], [z2p], [x3, summed]][D_X2Q])), "row")
        )
    late = [(1, [(j + 1, z2q, j - NEAR) for j in range(NEAR, 6)]), (2, [z1_rest])]
    late.append((-3, [(3 - j, x3, j) for j in range(4)]))
    ins = [z2q, x3, z1b if D_ZB else z1]
    if not D_KE:
        late.append((-1, rest_terms))
        ins.append(x1q)
    summed = stage(summed, KC, ins, late)
    summed = stage(summed, 0, [z3], [(3, [(j + 3, z3, j) for j in range(4)])])
    new_own, middle, rim_a, rim_b = call(
        functools.partial(last_kernel, dims),
        [
            ((rows, dims.wc * dims.bs), BF16),
            ((SX, EY), F32),
            ((M, EY), F32),
            ((M, EY), F32),
        ],
        [mask, squares, summed, *x2, xt, y_spread],
    )
    (new_density,) = call(
        functools.partial(order_kernel, dims), [(new_own.shape, BF16)], [new_own]
    )
    got_a = swap_partner(rim_a, "row")
    got_b = swap_other(rim_b, "row")
    center, rim_a, rim_b = call(
        row_rims_kernel,
        [((SX, SY), F32), ((SX, M), F32), ((SX, M), F32)],
        [middle, got_a, got_b],
    )
    got_a = swap_partner(rim_a, "col")
    got_b = swap_other(rim_b, "col")
    (grid_density,) = call(col_rims_kernel, [((SX, SY), F32)], [center, got_a, got_b])
    return new_density, grid_density


def solution(mesh):
    placed = (
        P("row", None),
        P("row", "col"),
        P("row", None),
        P("row", None),
        P("row"),
        P("row"),
        P("row", "col", None),
        P("row", "col"),
        P("row", "col"),
    )
    return jax.shard_map(
        shards,
        mesh=mesh,
        in_specs=placed,
        out_specs=(P("row", "col"), P("row", "col")),
        check_vma=False,
    )
```

```python
import functools

import jax
import jax.numpy as jnp
from jax import lax
from jax.experimental import pallas as pl
from jax.experimental.pallas import tpu as pltpu
from jax.sharding import PartitionSpec as P

HD = 3
SX = 128
SY = 128
M = 32
EX = SX + 2 * M
EY = SY + 2 * M
CHUNKS = 2 * HD + 1
NEAR = HD + 1
AHEAD = HD + 2
VMEM = pl.BlockSpec(memory_space=pltpu.VMEM)
SMEM = pl.BlockSpec(memory_space=pltpu.SMEM)
HBM = pl.BlockSpec(memory_space=pltpu.HBM)
F32 = jnp.float32
BF16 = jnp.bfloat16


class Dims:
    def __init__(self, pattern, x_basis, n_col):
        self.br, self.win = pattern.shape
        self.bs = x_basis.shape[0] // self.br
        self.n_col = n_col
        self.wc = self.win // n_col
        self.stride = self.br // n_col
        self.uw = self.stride * self.bs
        self.rows = self.br * self.bs


def block_mask(pattern_ref, block_row, slots, bs, dtype):
    lane = lax.broadcasted_iota(jnp.int32, (1, bs * len(slots)), 1)
    row = jnp.zeros((1, bs * len(slots)), jnp.int32)
    for place, slot in enumerate(slots):
        inside = (lane >= place * bs) & (lane < (place + 1) * bs)
        row = jnp.where(inside, pattern_ref[block_row, slot], row)
    return row.astype(F32).astype(dtype)


def own_slots(dims, chunk, column):
    return [dims.n_col * (chunk * dims.stride + s) + column for s in range(dims.stride)]


def mask_kernel(
    dims,
    pattern_hbm,
    density_hbm,
    x1a_ref,
    x1b_ref,
    *refs,
):
    z1_refs, refs = refs[:-8], refs[-8:]
    pattern_ref, tile_ref, kept_ref, pattern_sem, tile_sems, x1a_sem, x1b_sem, z1_sem = refs
    odd = lax.axis_index("row") % 2
    column = lax.axis_index("col")
    bs, uw = dims.bs, dims.uw
    wide = tile_ref.shape[2]
    fetch_pattern = pltpu.make_async_copy(pattern_hbm, pattern_ref, pattern_sem)
    fetch_pattern.start()
    fetches = []
    for part in range(tile_ref.shape[0]):
        cols = pl.ds(part * wide, wide)
        fetch = pltpu.make_async_copy(density_hbm.at[:, cols], tile_ref.at[part], tile_sems.at[part])
        fetch.start()
        fetches.append(fetch)
    fetch_pattern.wait()
    near, first = x1a_ref.shape[0], z1_refs[0].shape[0]

    def copies_of(chunk, lane_odd):
        own = chunk if lane_odd else CHUNKS - 1 - chunk
        sent = CHUNKS - 1 - own
        tile = kept_ref.at[chunk]
        found = [
            pltpu.make_async_copy(tile, x1a_ref.at[sent], x1a_sem.at[sent])
            if sent < near
            else pltpu.make_async_copy(tile, x1b_ref.at[sent - near], x1b_sem.at[sent - near])
        ]
        if own < 5:
            dest = z1_refs[0].at[own] if own < first else z1_refs[1].at[own - first]
            found.append(pltpu.make_async_copy(tile, dest, z1_sem.at[own]))
        return found

    arrived = 0
    for chunk in range(CHUNKS):
        part, start = divmod(chunk * uw, wide)
        if part == arrived:
            fetches[part].wait()
            arrived += 1
        for i in range(dims.br):
            rows = slice(i * bs, (i + 1) * bs)
            mask = block_mask(pattern_ref, i, own_slots(dims, chunk, column), bs, BF16)
            kept_ref[chunk, rows, :] = tile_ref[part, rows, start : start + uw] * mask
        for lane_odd in (0, 1):

            @pl.when(odd == lane_odd)
            def _():
                for copy in copies_of(chunk, lane_odd):
                    copy.start()

    for lane_odd in (0, 1):

        @pl.when(odd == lane_odd)
        def _():
            for chunk in range(CHUNKS):
                for copy in copies_of(chunk, lane_odd):
                    copy.wait()


def own_block_cols(dims, p2_ref, slot, column):
    pair = pl.multiple_of((dims.n_col * slot // 2 + column // 2) * 2 * dims.bs, 2 * dims.bs)
    wide = p2_ref[:, pl.ds(pair, 2 * dims.bs)].astype(F32)
    return jnp.where(column % 2 == 1, wide[:, dims.bs :], wide[:, : dims.bs])


def spread_kernel(dims, *refs):
    inputs, refs = refs[:7], refs[7:]
    xt_ref, y_ref, mask_ref, wide_ref = refs[:4]
    held, sems = refs[4:11], refs[11]
    copies = [
        pltpu.make_async_copy(source, dest, sems.at[at])
        for at, (source, dest) in enumerate(zip(inputs, held))
    ]
    for copy in copies:
        copy.start()
    for copy in copies:
        copy.wait()
    pattern_ref, x_offset_ref, x_extent_ref, y_offset_ref, y_extent_ref, x_basis_ref, y_basis_ref = held
    odd = lax.axis_index("row") % 2
    column = lax.axis_index("col")
    bs, br = dims.bs, dims.br
    width = br * bs
    for i in range(br):
        for block in range(CHUNKS):
            slots = [block * br + t for t in range(br)]
            mask = block_mask(pattern_ref, i, slots, bs, F32)
            wide_ref[i : i + 1, block * width : (block + 1) * width] = mask
    tx = y_basis_ref.shape[0]
    step = lax.broadcasted_iota(jnp.int32, (tx, EY), 0)
    cell = lax.broadcasted_iota(jnp.int32, (tx, EY), 1)
    for chunk in range(CHUNKS):
        place = jnp.where(odd == 1, chunk, CHUNKS - 1 - chunk)
        for i in range(br):
            slots = own_slots(dims, chunk, column)
            mask_ref[place, i : i + 1, :] = 2.0 * block_mask(pattern_ref, i, slots, bs, F32)
        for s in range(dims.stride):
            m = chunk * dims.stride + s
            hit = (cell == y_offset_ref[0, m] + step) & (step < y_extent_ref[0, m])
            spread = lax.dot_general(
                y_basis_ref[:, m * bs : (m + 1) * bs],
                hit.astype(F32).astype(BF16),
                (((0,), (0,)), ((), ())),
                preferred_element_type=F32,
            )
            y_ref[place, s * bs : (s + 1) * bs, :] = spread.astype(BF16)
    step = lax.broadcasted_iota(jnp.int32, (EX, tx), 1)
    cell = lax.broadcasted_iota(jnp.int32, (EX, tx), 0)
    for i in range(br):
        hit = (cell == x_offset_ref[i] + step) & (step < x_extent_ref[i])
        spread = jnp.dot(
            hit.astype(F32).astype(BF16),
            x_basis_ref[:, i * bs : (i + 1) * bs],
            preferred_element_type=F32,
        )
        xt_ref[:, i * bs : (i + 1) * bs] = spread.astype(BF16)


def square_kernel(dims, p2_ref, wide_ref, *refs):
    squares_ref, summed_ref = refs[3:5]
    for source, dest in zip(refs[:3], refs[5:]):
        dest[...] = source[...]
    odd = lax.axis_index("row") % 2
    column = lax.axis_index("col")
    bs, br = dims.bs, dims.br
    width = br * bs
    for block in range(CHUNKS):
        place = jnp.where(odd == 1, block, CHUNKS - 1 - block)
        cols = slice(block * width, (block + 1) * width)
        for i in range(br):
            rows = slice(i * bs, (i + 1) * bs)
            squares_ref[place, rows, :] = p2_ref[rows, cols] * wide_ref[i : i + 1, cols].astype(BF16)
    for chunk in range(CHUNKS):
        place = jnp.where(odd == 1, chunk, CHUNKS - 1 - chunk)
        parts = [
            own_block_cols(dims, p2_ref, chunk * dims.stride + s, column)
            for s in range(dims.stride)
        ]
        own = parts[0] if len(parts) == 1 else jnp.concatenate(parts, axis=1)
        summed_ref[place] = 1.5 * own


def paired(terms):
    return [terms[at : at + 2] for at in range(0, len(terms), 2)]


def add_products(square, terms, summed_ref):
    for group in paired(terms):
        tiles = [tile[...] for _, tile in group]
        wide = tiles[0] if len(tiles) == 1 else jnp.concatenate(tiles, axis=1)
        product = jnp.dot(square, wide, preferred_element_type=F32)
        uw = tiles[0].shape[1]
        for at, (place, _) in enumerate(group):
            summed_ref[place] -= product[:, at * uw : (at + 1) * uw]


def first_kernel(squares_ref, before_ref, x1a_ref, x1b_ref, summed_ref):
    summed_ref[...] = before_ref[...]
    own = lambda j: x1a_ref.at[j] if j < NEAR else x1b_ref.at[j - NEAR]
    add_products(
        squares_ref[HD], [(k, own(CHUNKS - 1 - k)) for k in range(CHUNKS)], summed_ref
    )


def stage_kernel(terms, squares_ref, before_ref, *refs):
    summed_ref = refs[-1]
    summed_ref[...] = before_ref[...]
    for distance, pairs in terms:
        add_products(
            squares_ref[HD + distance],
            [(place, refs[which].at[at]) for place, which, at in pairs],
            summed_ref,
        )


def last_kernel(dims, mask_ref, squares_ref, before_ref, x2p_ref, x2q_ref, z3_ref, z1b_ref, *refs):
    xt_ref, y_ref, new_ref, middle_ref, rim_a_ref, rim_b_ref = refs
    odd = lax.axis_index("row") % 2
    bs, uw = dims.bs, dims.uw

    def product(distance, *tiles):
        wide = tiles[0] if len(tiles) == 1 else jnp.concatenate(tiles, axis=1)
        return jnp.dot(squares_ref[HD + distance], wide, preferred_element_type=F32)

    def finish(k, total):
        for i in range(dims.br):
            rows = slice(i * bs, (i + 1) * bs)
            kept = total[rows] * mask_ref[k, i : i + 1, :]
            new_ref[rows, k * uw : (k + 1) * uw] = kept.astype(BF16)

    x2 = [x2p_ref[j] for j in range(NEAR)] + [x2q_ref[0]]
    low = product(-2, x2[4], x2[3])
    mid = product(-2, x2[1], x2[0]) + product(3, z3_ref[0], z3_ref[1])
    high = product(3, z3_ref[2], z3_ref[3])
    finish(0, before_ref[0] - low[:, :uw])
    finish(1, before_ref[1] - low[:, uw:])
    finish(2, before_ref[2] - product(-2, x2[2]))
    finish(3, before_ref[3] - mid[:, :uw])
    finish(4, before_ref[4] - mid[:, uw:])
    finish(5, before_ref[5] - high[:, :uw])
    finish(6, before_ref[6] - high[:, uw:] - product(2, z1b_ref[0]))
    half = jnp.dot(
        new_ref[...], y_ref[...].reshape(CHUNKS * uw, EY), preferred_element_type=F32
    )
    extended = jnp.dot(xt_ref[...], half.astype(BF16), preferred_element_type=F32)
    middle_ref[...] = extended[M : M + SX]
    lower, upper = extended[:M], extended[SX + M :]
    rim_a_ref[...] = jnp.where(odd == 1, lower, upper)
    rim_b_ref[...] = jnp.where(odd == 1, upper, lower)


def order_kernel(dims, own_ref, new_ref):
    odd = lax.axis_index("row") % 2
    uw = dims.uw

    @pl.when(odd == 1)
    def _():
        new_ref[...] = own_ref[...]

    @pl.when(odd == 0)
    def _():
        for k in range(CHUNKS):
            at = CHUNKS - 1 - k
            new_ref[:, at * uw : (at + 1) * uw] = own_ref[:, k * uw : (k + 1) * uw]


def row_rims_kernel(middle_ref, got_a_ref, got_b_ref, center_ref, rim_a_ref, rim_b_ref):
    odd = lax.axis_index("row") % 2
    col_odd = lax.axis_index("col") % 2
    got_a, got_b = got_a_ref[...], got_b_ref[...]
    low = jnp.where(odd == 1, got_a, got_b)
    high = jnp.where(odd == 1, got_b, got_a)
    interior = jnp.concatenate(
        [middle_ref[:M] + low, middle_ref[M : SX - M], middle_ref[SX - M :] + high], axis=0
    )
    center_ref[...] = interior[:, M : M + SY]
    lower, upper = interior[:, :M], interior[:, SY + M :]
    rim_a_ref[...] = jnp.where(col_odd == 1, lower, upper)
    rim_b_ref[...] = jnp.where(col_odd == 1, upper, lower)


def col_rims_kernel(center_ref, got_a_ref, got_b_ref, grid_ref):
    col_odd = lax.axis_index("col") % 2
    got_a, got_b = got_a_ref[...], got_b_ref[...]
    low = jnp.where(col_odd == 1, got_a, got_b)
    high = jnp.where(col_odd == 1, got_b, got_a)
    none = jnp.zeros((SX, SY - 2 * M), F32)
    grid_ref[...] = center_ref[...] + jnp.concatenate([low, none, high], axis=1)


def swap_partner(value, axis):
    count = lax.axis_size(axis)
    return lax.ppermute(value, axis, [(s, s ^ 1) for s in range(count)])


def swap_other(value, axis):
    count = lax.axis_size(axis)
    pairs = [(s, (s - 1) % count if s % 2 == 0 else (s + 1) % count) for s in range(count)]
    return lax.ppermute(value, axis, pairs)


def shift_level(value):
    count = lax.axis_size("row")
    pairs = [(s, (s + 2) % count if s % 2 == 0 else (s - 2) % count) for s in range(count)]
    return lax.ppermute(value, "row", pairs)


def after(value, *others):
    return lax.optimization_barrier((value,) + others)[0]


def call(kernel, outs, ins, scratch=(), beside=0, stay=(), outs_stay=False, limit=24):
    shapes = [jax.ShapeDtypeStruct(shape, dtype) for shape, dtype in outs]
    specs = [
        HBM
        if at in stay
        else SMEM
        if jnp.issubdtype(value.dtype, jnp.integer)
        else VMEM
        for at, value in enumerate(ins)
    ]
    moved = sum(value.size * value.dtype.itemsize for value in list(ins) + shapes)
    return pl.pallas_call(
        kernel,
        out_shape=shapes,
        in_specs=specs,
        out_specs=[HBM if outs_stay else VMEM] * len(shapes),
        scratch_shapes=list(scratch),
        compiler_params=pltpu.CompilerParams(vmem_limit_bytes=limit * 2**20),
        cost_estimate=pl.CostEstimate(
            flops=beside * 10**9, bytes_accessed=moved, transcendentals=0
        ),
    )(*ins)


def shards(p2_panel, density, pattern, x_basis, x_offset, x_extent, y_basis, y_offset, y_extent):
    dims = Dims(pattern, x_basis, lax.axis_size("col"))
    rows, uw = dims.rows, dims.uw
    chunks = lambda count: ((count, rows, uw), BF16)
    total = ((CHUNKS, rows, uw), F32)

    parts = CHUNKS if uw % 128 == 0 else 1
    own_p, own_q, own_z, own_zb = call(
        functools.partial(mask_kernel, dims),
        [chunks(NEAR), chunks(CHUNKS - NEAR), chunks(NEAR), chunks(AHEAD - NEAR)],
        [pattern, density],
        scratch=[
            pltpu.SMEM(pattern.shape, jnp.int32),
            pltpu.VMEM((parts, rows, CHUNKS * uw // parts), BF16),
            pltpu.VMEM((CHUNKS, rows, uw), BF16),
            pltpu.SemaphoreType.DMA(()),
            pltpu.SemaphoreType.DMA((parts,)),
            pltpu.SemaphoreType.DMA((NEAR,)),
            pltpu.SemaphoreType.DMA((CHUNKS - NEAR,)),
            pltpu.SemaphoreType.DMA((AHEAD,)),
        ],
        stay=(0, 1),
        outs_stay=True,
        limit=60,
    )
    x1p = swap_partner(own_p, "row")
    z1 = shift_level(own_z)
    x1q = swap_partner(own_q, "row")

    small = [pattern, x_offset, x_extent, y_offset, y_extent, x_basis.T, y_basis[0].T]
    xt, y_spread, mask, wide = call(
        functools.partial(spread_kernel, dims),
        [
            ((EX, rows), BF16),
            ((CHUNKS, uw, EY), BF16),
            ((CHUNKS, dims.br, uw), F32),
            ((dims.br, dims.win * dims.bs), F32),
        ],
        small,
        scratch=[
            (pltpu.SMEM if jnp.issubdtype(value.dtype, jnp.integer) else pltpu.VMEM)(
                value.shape, value.dtype
            )
            for value in small
        ]
        + [pltpu.SemaphoreType.DMA((len(small),))],
        stay=range(len(small)),
        limit=60,
        beside=6,
    )
    kept = [xt, y_spread, mask]
    squares, summed, xt, y_spread, mask = call(
        functools.partial(square_kernel, dims),
        [((CHUNKS, rows, rows), BF16), total] + [(value.shape, value.dtype) for value in kept],
        [p2_panel, wide] + kept,
        beside=1,
    )
    ready = summed

    def stage(summed, terms, beside=0):
        tiles = []
        for _, pairs in terms:
            for _, tile, _ in pairs:
                if not any(tile is known for known in tiles):
                    tiles.append(tile)
        spot = lambda tile: next(at for at, known in enumerate(tiles) if known is tile)
        listed = [(d, [(place, spot(tile), at) for place, tile, at in pairs]) for d, pairs in terms]
        return call(
            functools.partial(stage_kernel, listed),
            [total],
            [squares, summed] + tiles,
            beside=beside,
        )[0]

    (summed,) = call(first_kernel, [total], [squares, summed, own_p, own_q])
    z2p = shift_level(after(x1p, ready))
    x3 = swap_partner(z1, "row")
    z2q = shift_level(x1q[: 2 * HD - NEAR])
    z1b = shift_level(after(own_zb, z1))
    partner = [(j - 1, x1p, j) for j in range(1, NEAR)]
    partner += [(j - 1, x1q, j - NEAR) for j in range(NEAR, CHUNKS)]
    summed = stage(
        summed, [(-1, partner), (2, [(j + 2, z1, j) for j in range(NEAR)])], beside=3
    )
    x2p = swap_partner(after(z2p, summed), "row")
    z3 = shift_level(z2p)
    summed = stage(summed, [(1, [(j + 1, z2p, j) for j in range(NEAR)])])
    x2q = swap_partner(after(z2q[: AHEAD - NEAR], z2p), "row")
    summed = stage(
        summed,
        [
            (1, [(j + 1, z2q, j - NEAR) for j in range(NEAR, 2 * HD)]),
            (-3, [(3 - j, x3, j) for j in range(NEAR)]),
        ],
        beside=4,
    )
    new_own, middle, rim_a, rim_b = call(
        functools.partial(last_kernel, dims),
        [
            ((rows, dims.wc * dims.bs), BF16),
            ((SX, EY), F32),
            ((M, EY), F32),
            ((M, EY), F32),
        ],
        [mask, squares, summed, x2p, x2q, z3, z1b, xt, y_spread],
    )
    (new_density,) = call(
        functools.partial(order_kernel, dims), [(new_own.shape, BF16)], [new_own]
    )
    got_a = swap_partner(rim_a, "row")
    got_b = swap_other(rim_b, "row")
    center, rim_a, rim_b = call(
        row_rims_kernel,
        [((SX, SY), F32), ((SX, M), F32), ((SX, M), F32)],
        [middle, got_a, got_b],
    )
    got_a = swap_partner(rim_a, "col")
    got_b = swap_other(rim_b, "col")
    (grid_density,) = call(col_rims_kernel, [((SX, SY), F32)], [center, got_a, got_b])
    return new_density, grid_density


def solution(mesh):
    placed = (
        P("row", None),
        P("row", "col"),
        P("row", None),
        P("row", None),
        P("row"),
        P("row"),
        P("row", "col", None),
        P("row", "col"),
        P("row", "col"),
    )
    return jax.shard_map(
        shards,
        mesh=mesh,
        in_specs=placed,
        out_specs=(P("row", "col"), P("row", "col")),
        check_vma=False,
    )
```

```python
import functools

import jax
import jax.numpy as jnp
from jax import lax
from jax.experimental import pallas as pl
from jax.experimental.pallas import tpu as pltpu
from jax.sharding import PartitionSpec as P

HD = 3
SX = 128
SY = 128
M = 32
EX = SX + 2 * M
EY = SY + 2 * M
CHUNKS = 2 * HD + 1
NEAR = HD + 1
AHEAD = HD + 2
VMEM = pl.BlockSpec(memory_space=pltpu.VMEM)
SMEM = pl.BlockSpec(memory_space=pltpu.SMEM)
HBM = pl.BlockSpec(memory_space=pltpu.HBM)
F32 = jnp.float32
BF16 = jnp.bfloat16


class Dims:
    def __init__(self, pattern, x_basis, n_col):
        self.br, self.win = pattern.shape
        self.bs = x_basis.shape[0] // self.br
        self.n_col = n_col
        self.wc = self.win // n_col
        self.stride = self.br // n_col
        self.uw = self.stride * self.bs
        self.rows = self.br * self.bs


def block_mask(pattern_ref, block_row, slots, bs, dtype):
    lane = lax.broadcasted_iota(jnp.int32, (1, bs * len(slots)), 1)
    row = jnp.zeros((1, bs * len(slots)), jnp.int32)
    for place, slot in enumerate(slots):
        inside = (lane >= place * bs) & (lane < (place + 1) * bs)
        row = jnp.where(inside, pattern_ref[block_row, slot], row)
    return row.astype(F32).astype(dtype)


def own_slots(dims, chunk, column):
    return [dims.n_col * (chunk * dims.stride + s) + column for s in range(dims.stride)]


def mask_kernel(
    dims,
    pattern_hbm,
    density_hbm,
    x1a_ref,
    x1b_ref,
    *refs,
):
    z1_refs, refs = refs[:-8], refs[-8:]
    pattern_ref, tile_ref, kept_ref, pattern_sem, tile_sems, x1a_sem, x1b_sem, z1_sem = refs
    odd = lax.axis_index("row") % 2
    column = lax.axis_index("col")
    bs, uw = dims.bs, dims.uw
    wide = tile_ref.shape[2]
    fetch_pattern = pltpu.make_async_copy(pattern_hbm, pattern_ref, pattern_sem)
    fetch_pattern.start()
    fetches = []
    for part in range(tile_ref.shape[0]):
        cols = pl.ds(part * wide, wide)
        fetch = pltpu.make_async_copy(density_hbm.at[:, cols], tile_ref.at[part], tile_sems.at[part])
        fetch.start()
        fetches.append(fetch)
    fetch_pattern.wait()
    near, first = x1a_ref.shape[0], z1_refs[0].shape[0]

    def copies_of(chunk, lane_odd):
        own = chunk if lane_odd else CHUNKS - 1 - chunk
        sent = CHUNKS - 1 - own
        tile = kept_ref.at[chunk]
        found = [
            pltpu.make_async_copy(tile, x1a_ref.at[sent], x1a_sem.at[sent])
            if sent < near
            else pltpu.make_async_copy(tile, x1b_ref.at[sent - near], x1b_sem.at[sent - near])
        ]
        if own < 5:
            dest = z1_refs[0].at[own] if own < first else z1_refs[1].at[own - first]
            found.append(pltpu.make_async_copy(tile, dest, z1_sem.at[own]))
        return found

    arrived = 0
    for chunk in range(CHUNKS):
        part, start = divmod(chunk * uw, wide)
        if part == arrived:
            fetches[part].wait()
            arrived += 1
        for i in range(dims.br):
            rows = slice(i * bs, (i + 1) * bs)
            mask = block_mask(pattern_ref, i, own_slots(dims, chunk, column), bs, BF16)
            kept_ref[chunk, rows, :] = tile_ref[part, rows, start : start + uw] * mask
        for lane_odd in (0, 1):

            @pl.when(odd == lane_odd)
            def _():
                for copy in copies_of(chunk, lane_odd):
                    copy.start()

    for lane_odd in (0, 1):

        @pl.when(odd == lane_odd)
        def _():
            for chunk in range(CHUNKS):
                for copy in copies_of(chunk, lane_odd):
                    copy.wait()


def own_block_cols(dims, p2_ref, slot, column):
    pair = pl.multiple_of((dims.n_col * slot // 2 + column // 2) * 2 * dims.bs, 2 * dims.bs)
    wide = p2_ref[:, pl.ds(pair, 2 * dims.bs)].astype(F32)
    return jnp.where(column % 2 == 1, wide[:, dims.bs :], wide[:, : dims.bs])


def spread_kernel(dims, *refs):
    inputs, refs = refs[:7], refs[7:]
    xt_ref, y_ref, mask_ref, wide_ref = refs[:4]
    held, sems = refs[4:11], refs[11]
    copies = [
        pltpu.make_async_copy(source, dest, sems.at[at])
        for at, (source, dest) in enumerate(zip(inputs, held))
    ]
    for copy in copies:
        copy.start()
    for copy in copies:
        copy.wait()
    pattern_ref, x_offset_ref, x_extent_ref, y_offset_ref, y_extent_ref, x_basis_ref, y_basis_ref = held
    odd = lax.axis_index("row") % 2
    column = lax.axis_index("col")
    bs, br = dims.bs, dims.br
    width = br * bs
    for i in range(br):
        for block in range(CHUNKS):
            slots = [block * br + t for t in range(br)]
            mask = block_mask(pattern_ref, i, slots, bs, F32)
            wide_ref[i : i + 1, block * width : (block + 1) * width] = mask
    tx = y_basis_ref.shape[0]
    step = lax.broadcasted_iota(jnp.int32, (tx, EY), 0)
    cell = lax.broadcasted_iota(jnp.int32, (tx, EY), 1)
    for chunk in range(CHUNKS):
        place = jnp.where(odd == 1, chunk, CHUNKS - 1 - chunk)
        for i in range(br):
            slots = own_slots(dims, chunk, column)
            mask_ref[place, i : i + 1, :] = 2.0 * block_mask(pattern_ref, i, slots, bs, F32)
        for s in range(dims.stride):
            m = chunk * dims.stride + s
            hit = (cell == y_offset_ref[0, m] + step) & (step < y_extent_ref[0, m])
            spread = lax.dot_general(
                y_basis_ref[:, m * bs : (m + 1) * bs],
                hit.astype(F32).astype(BF16),
                (((0,), (0,)), ((), ())),
                preferred_element_type=F32,
            )
            y_ref[place, s * bs : (s + 1) * bs, :] = spread.astype(BF16)
    step = lax.broadcasted_iota(jnp.int32, (EX, tx), 1)
    cell = lax.broadcasted_iota(jnp.int32, (EX, tx), 0)
    for i in range(br):
        hit = (cell == x_offset_ref[i] + step) & (step < x_extent_ref[i])
        spread = jnp.dot(
            hit.astype(F32).astype(BF16),
            x_basis_ref[:, i * bs : (i + 1) * bs],
            preferred_element_type=F32,
        )
        xt_ref[:, i * bs : (i + 1) * bs] = spread.astype(BF16)


def square_kernel(dims, p2_ref, wide_ref, *refs):
    squares_ref, summed_ref = refs[3:5]
    for source, dest in zip(refs[:3], refs[5:]):
        dest[...] = source[...]
    odd = lax.axis_index("row") % 2
    column = lax.axis_index("col")
    bs, br = dims.bs, dims.br
    width = br * bs
    for block in range(CHUNKS):
        place = jnp.where(odd == 1, block, CHUNKS - 1 - block)
        cols = slice(block * width, (block + 1) * width)
        for i in range(br):
            rows = slice(i * bs, (i + 1) * bs)
            squares_ref[place, rows, :] = p2_ref[rows, cols] * wide_ref[i : i + 1, cols].astype(BF16)
    for chunk in range(CHUNKS):
        place = jnp.where(odd == 1, chunk, CHUNKS - 1 - chunk)
        parts = [
            own_block_cols(dims, p2_ref, chunk * dims.stride + s, column)
            for s in range(dims.stride)
        ]
        own = parts[0] if len(parts) == 1 else jnp.concatenate(parts, axis=1)
        summed_ref[place] = 1.5 * own


def paired(terms):
    return [terms[at : at + 2] for at in range(0, len(terms), 2)]


def add_products(square, terms, summed_ref):
    for group in paired(terms):
        tiles = [tile[...] for _, tile in group]
        wide = tiles[0] if len(tiles) == 1 else jnp.concatenate(tiles, axis=1)
        product = jnp.dot(square, wide, preferred_element_type=F32)
        uw = tiles[0].shape[1]
        for at, (place, _) in enumerate(group):
            summed_ref[place] -= product[:, at * uw : (at + 1) * uw]


def first_kernel(squares_ref, before_ref, x1a_ref, x1b_ref, summed_ref):
    summed_ref[...] = before_ref[...]
    own = lambda j: x1a_ref.at[j] if j < NEAR else x1b_ref.at[j - NEAR]
    add_products(
        squares_ref[HD], [(k, own(CHUNKS - 1 - k)) for k in range(CHUNKS)], summed_ref
    )


def stage_kernel(terms, squares_ref, before_ref, *refs):
    summed_ref = refs[-1]
    summed_ref[...] = before_ref[...]
    for distance, pairs in terms:
        add_products(
            squares_ref[HD + distance],
            [(place, refs[which].at[at]) for place, which, at in pairs],
            summed_ref,
        )


def finish(mask_ref, k, total, new_ref, at):
    br, uw = mask_ref.shape[1:]
    bs = total.shape[0] // br
    for i in range(br):
        rows = slice(i * bs, (i + 1) * bs)
        kept = total[rows] * mask_ref[k, i : i + 1, :]
        new_ref[rows, at * uw : (at + 1) * uw] = kept.astype(BF16)


def inner_kernel(
    mask_ref, squares_ref, before_ref, x2p_ref, z3_ref, y_ref, new_ref, half_ref, edges_ref
):
    uw = edges_ref.shape[2]

    def product(distance, *tiles):
        wide = jnp.concatenate(tiles, axis=1)
        return jnp.dot(squares_ref[HD + distance], wide, preferred_element_type=F32)

    low = product(-2, x2p_ref[3], x2p_ref[2])
    mid = product(-2, x2p_ref[1], x2p_ref[0]) + product(3, z3_ref[0], z3_ref[1])
    high = product(3, z3_ref[2], z3_ref[3])
    parts = [low[:, :uw], low[:, uw:], mid[:, :uw], mid[:, uw:], high[:, :uw]]
    for at, part in enumerate(parts):
        finish(mask_ref, at + 1, before_ref[at + 1] - part, new_ref, at)
    edges_ref[0] = before_ref[0]
    edges_ref[1] = before_ref[CHUNKS - 1] - high[:, uw:]
    inner = y_ref[1 : CHUNKS - 1].reshape((CHUNKS - 2) * uw, EY)
    half_ref[...] = jnp.dot(new_ref[...], inner, preferred_element_type=F32)


def last_kernel(
    mask_ref,
    squares_ref,
    edges_ref,
    x2q_ref,
    z1b_ref,
    xt_ref,
    y_ref,
    half_ref,
    new_ref,
    middle_ref,
    rim_a_ref,
    rim_b_ref,
):
    odd = lax.axis_index("row") % 2
    product = lambda d, tile: jnp.dot(squares_ref[HD + d], tile, preferred_element_type=F32)
    finish(mask_ref, 0, edges_ref[0] - product(-2, x2q_ref[0]), new_ref, 0)
    finish(mask_ref, CHUNKS - 1, edges_ref[1] - product(2, z1b_ref[0]), new_ref, 1)
    outer = jnp.concatenate([y_ref[0], y_ref[CHUNKS - 1]], axis=0)
    half = half_ref[...] + jnp.dot(new_ref[...], outer, preferred_element_type=F32)
    extended = jnp.dot(xt_ref[...], half.astype(BF16), preferred_element_type=F32)
    middle_ref[...] = extended[M : M + SX]
    lower, upper = extended[:M], extended[SX + M :]
    rim_a_ref[...] = jnp.where(odd == 1, lower, upper)
    rim_b_ref[...] = jnp.where(odd == 1, upper, lower)


def order_kernel(inner_ref, edges_ref, new_ref):
    odd = lax.axis_index("row") % 2
    uw = edges_ref.shape[1] // 2

    @pl.when(odd == 1)
    def _():
        new_ref[:, :uw] = edges_ref[:, :uw]
        new_ref[:, uw : (CHUNKS - 1) * uw] = inner_ref[...]
        new_ref[:, (CHUNKS - 1) * uw :] = edges_ref[:, uw:]

    @pl.when(odd == 0)
    def _():
        new_ref[:, :uw] = edges_ref[:, uw:]
        for at in range(CHUNKS - 2):
            place = CHUNKS - 2 - at
            new_ref[:, place * uw : (place + 1) * uw] = inner_ref[:, at * uw : (at + 1) * uw]
        new_ref[:, (CHUNKS - 1) * uw :] = edges_ref[:, :uw]


def row_rims_kernel(middle_ref, got_a_ref, got_b_ref, center_ref, rim_a_ref, rim_b_ref):
    odd = lax.axis_index("row") % 2
    col_odd = lax.axis_index("col") % 2
    got_a, got_b = got_a_ref[...], got_b_ref[...]
    low = jnp.where(odd == 1, got_a, got_b)
    high = jnp.where(odd == 1, got_b, got_a)
    interior = jnp.concatenate(
        [middle_ref[:M] + low, middle_ref[M : SX - M], middle_ref[SX - M :] + high], axis=0
    )
    center_ref[...] = interior[:, M : M + SY]
    lower, upper = interior[:, :M], interior[:, SY + M :]
    rim_a_ref[...] = jnp.where(col_odd == 1, lower, upper)
    rim_b_ref[...] = jnp.where(col_odd == 1, upper, lower)


def col_rims_kernel(center_ref, got_a_ref, got_b_ref, grid_ref):
    col_odd = lax.axis_index("col") % 2
    got_a, got_b = got_a_ref[...], got_b_ref[...]
    low = jnp.where(col_odd == 1, got_a, got_b)
    high = jnp.where(col_odd == 1, got_b, got_a)
    none = jnp.zeros((SX, SY - 2 * M), F32)
    grid_ref[...] = center_ref[...] + jnp.concatenate([low, none, high], axis=1)


def swap_partner(value, axis):
    count = lax.axis_size(axis)
    return lax.ppermute(value, axis, [(s, s ^ 1) for s in range(count)])


def swap_other(value, axis):
    count = lax.axis_size(axis)
    pairs = [(s, (s - 1) % count if s % 2 == 0 else (s + 1) % count) for s in range(count)]
    return lax.ppermute(value, axis, pairs)


def shift_level(value):
    count = lax.axis_size("row")
    pairs = [(s, (s + 2) % count if s % 2 == 0 else (s - 2) % count) for s in range(count)]
    return lax.ppermute(value, "row", pairs)


def after(value, *others):
    return lax.optimization_barrier((value,) + others)[0]


def call(kernel, outs, ins, scratch=(), beside=0, stay=(), outs_stay=False, limit=24):
    shapes = [jax.ShapeDtypeStruct(shape, dtype) for shape, dtype in outs]
    specs = [
        HBM
        if at in stay
        else SMEM
        if jnp.issubdtype(value.dtype, jnp.integer)
        else VMEM
        for at, value in enumerate(ins)
    ]
    moved = sum(value.size * value.dtype.itemsize for value in list(ins) + shapes)
    return pl.pallas_call(
        kernel,
        out_shape=shapes,
        in_specs=specs,
        out_specs=[HBM if outs_stay else VMEM] * len(shapes),
        scratch_shapes=list(scratch),
        compiler_params=pltpu.CompilerParams(vmem_limit_bytes=limit * 2**20),
        cost_estimate=pl.CostEstimate(
            flops=beside * 10**9, bytes_accessed=moved, transcendentals=0
        ),
    )(*ins)


def shards(p2_panel, density, pattern, x_basis, x_offset, x_extent, y_basis, y_offset, y_extent):
    dims = Dims(pattern, x_basis, lax.axis_size("col"))
    rows, uw = dims.rows, dims.uw
    chunks = lambda count: ((count, rows, uw), BF16)
    total = ((CHUNKS, rows, uw), F32)

    parts = CHUNKS if uw % 128 == 0 else 1
    own_p, own_q, own_z, own_zb = call(
        functools.partial(mask_kernel, dims),
        [chunks(NEAR), chunks(CHUNKS - NEAR), chunks(NEAR), chunks(AHEAD - NEAR)],
        [pattern, density],
        scratch=[
            pltpu.SMEM(pattern.shape, jnp.int32),
            pltpu.VMEM((parts, rows, CHUNKS * uw // parts), BF16),
            pltpu.VMEM((CHUNKS, rows, uw), BF16),
            pltpu.SemaphoreType.DMA(()),
            pltpu.SemaphoreType.DMA((parts,)),
            pltpu.SemaphoreType.DMA((NEAR,)),
            pltpu.SemaphoreType.DMA((CHUNKS - NEAR,)),
            pltpu.SemaphoreType.DMA((AHEAD,)),
        ],
        stay=(0, 1),
        outs_stay=True,
        limit=60,
    )
    x1p = swap_partner(own_p, "row")
    z1 = shift_level(own_z)
    x1q = swap_partner(own_q, "row")

    small = [pattern, x_offset, x_extent, y_offset, y_extent, x_basis.T, y_basis[0].T]
    xt, y_spread, mask, wide = call(
        functools.partial(spread_kernel, dims),
        [
            ((EX, rows), BF16),
            ((CHUNKS, uw, EY), BF16),
            ((CHUNKS, dims.br, uw), F32),
            ((dims.br, dims.win * dims.bs), F32),
        ],
        small,
        scratch=[
            (pltpu.SMEM if jnp.issubdtype(value.dtype, jnp.integer) else pltpu.VMEM)(
                value.shape, value.dtype
            )
            for value in small
        ]
        + [pltpu.SemaphoreType.DMA((len(small),))],
        stay=range(len(small)),
        limit=60,
        beside=6,
    )
    kept = [xt, y_spread, mask]
    squares, summed, xt, y_spread, mask = call(
        functools.partial(square_kernel, dims),
        [((CHUNKS, rows, rows), BF16), total] + [(value.shape, value.dtype) for value in kept],
        [p2_panel, wide] + kept,
        beside=1,
    )
    ready = summed

    def stage(summed, terms, beside=0):
        tiles = []
        for _, pairs in terms:
            for _, tile, _ in pairs:
                if not any(tile is known for known in tiles):
                    tiles.append(tile)
        spot = lambda tile: next(at for at, known in enumerate(tiles) if known is tile)
        listed = [(d, [(place, spot(tile), at) for place, tile, at in pairs]) for d, pairs in terms]
        return call(
            functools.partial(stage_kernel, listed),
            [total],
            [squares, summed] + tiles,
            beside=beside,
        )[0]

    (summed,) = call(first_kernel, [total], [squares, summed, own_p, own_q])
    z2p = shift_level(after(x1p, ready))
    x3 = swap_partner(z1, "row")
    z2q = shift_level(x1q[: 2 * HD - NEAR])
    z1b = shift_level(after(own_zb, z1))
    partner = [(j - 1, x1p, j) for j in range(1, NEAR)]
    partner += [(j - 1, x1q, j - NEAR) for j in range(NEAR, CHUNKS)]
    summed = stage(
        summed, [(-1, partner), (2, [(j + 2, z1, j) for j in range(NEAR)])], beside=3
    )
    x2p = swap_partner(after(z2p, summed), "row")
    z3 = shift_level(z2p)
    summed = stage(summed, [(1, [(j + 1, z2p, j) for j in range(NEAR)])])
    x2q = swap_partner(after(z2q[: AHEAD - NEAR], z2p), "row")
    summed = stage(
        summed,
        [
            (1, [(j + 1, z2q, j - NEAR) for j in range(NEAR, 2 * HD)]),
            (-3, [(3 - j, x3, j) for j in range(NEAR)]),
        ],
        beside=4,
    )
    new_inner, half, edges = call(
        inner_kernel,
        [((rows, (CHUNKS - 2) * uw), BF16), ((rows, EY), F32), ((2, rows, uw), F32)],
        [mask, squares, summed, x2p, z3, y_spread],
        beside=0,
    )
    new_edges, middle, rim_a, rim_b = call(
        last_kernel,
        [((rows, 2 * uw), BF16), ((SX, EY), F32), ((M, EY), F32), ((M, EY), F32)],
        [mask, squares, edges, x2q, z1b, xt, y_spread, half],
    )
    (new_density,) = call(
        order_kernel, [((rows, dims.wc * dims.bs), BF16)], [new_inner, new_edges]
    )
    got_a = swap_partner(rim_a, "row")
    got_b = swap_other(rim_b, "row")
    center, rim_a, rim_b = call(
        row_rims_kernel,
        [((SX, SY), F32), ((SX, M), F32), ((SX, M), F32)],
        [after(middle, new_density), got_a, got_b],
    )
    got_a = swap_partner(rim_a, "col")
    got_b = swap_other(rim_b, "col")
    (grid_density,) = call(col_rims_kernel, [((SX, SY), F32)], [center, got_a, got_b])
    return new_density, grid_density


def solution(mesh):
    placed = (
        P("row", None),
        P("row", "col"),
        P("row", None),
        P("row", None),
        P("row"),
        P("row"),
        P("row", "col", None),
        P("row", "col"),
        P("row", "col"),
    )
    return jax.shard_map(
        shards,
        mesh=mesh,
        in_specs=placed,
        out_specs=(P("row", "col"), P("row", "col")),
        check_vma=False,
    )
```

```python
import functools

import jax
import jax.numpy as jnp
from jax import lax
from jax.experimental import pallas as pl
from jax.experimental.pallas import tpu as pltpu
from jax.sharding import PartitionSpec as P

HD = 3
SX = 128
SY = 128
M = 32
EX = SX + 2 * M
EY = SY + 2 * M
CHUNKS = 2 * HD + 1
NEAR = HD + 1
AHEAD = HD + 2
VMEM = pl.BlockSpec(memory_space=pltpu.VMEM)
SMEM = pl.BlockSpec(memory_space=pltpu.SMEM)
HBM = pl.BlockSpec(memory_space=pltpu.HBM)
F32 = jnp.float32
BF16 = jnp.bfloat16


class Dims:
    def __init__(self, pattern, x_basis, n_col):
        self.br, self.win = pattern.shape
        self.bs = x_basis.shape[0] // self.br
        self.n_col = n_col
        self.wc = self.win // n_col
        self.stride = self.br // n_col
        self.uw = self.stride * self.bs
        self.rows = self.br * self.bs


def block_mask(pattern_ref, block_row, slots, bs, dtype):
    lane = lax.broadcasted_iota(jnp.int32, (1, bs * len(slots)), 1)
    row = jnp.zeros((1, bs * len(slots)), jnp.int32)
    for place, slot in enumerate(slots):
        inside = (lane >= place * bs) & (lane < (place + 1) * bs)
        row = jnp.where(inside, pattern_ref[block_row, slot], row)
    return row.astype(F32).astype(dtype)


def own_slots(dims, chunk, column):
    return [dims.n_col * (chunk * dims.stride + s) + column for s in range(dims.stride)]


def mask_kernel(
    dims,
    pattern_hbm,
    density_hbm,
    x1a_ref,
    x1b_ref,
    *refs,
):
    z1_refs, refs = refs[:-8], refs[-8:]
    pattern_ref, tile_ref, kept_ref, pattern_sem, tile_sems, x1a_sem, x1b_sem, z1_sem = refs
    odd = lax.axis_index("row") % 2
    column = lax.axis_index("col")
    bs, uw = dims.bs, dims.uw
    wide = tile_ref.shape[2]
    fetch_pattern = pltpu.make_async_copy(pattern_hbm, pattern_ref, pattern_sem)
    fetch_pattern.start()
    fetches = []
    for part in range(tile_ref.shape[0]):
        cols = pl.ds(part * wide, wide)
        fetch = pltpu.make_async_copy(density_hbm.at[:, cols], tile_ref.at[part], tile_sems.at[part])
        fetch.start()
        fetches.append(fetch)
    fetch_pattern.wait()
    near, first = x1a_ref.shape[0], z1_refs[0].shape[0]

    def copies_of(chunk, lane_odd):
        own = chunk if lane_odd else CHUNKS - 1 - chunk
        sent = CHUNKS - 1 - own
        tile = kept_ref.at[chunk]
        found = [
            pltpu.make_async_copy(tile, x1a_ref.at[sent], x1a_sem.at[sent])
            if sent < near
            else pltpu.make_async_copy(tile, x1b_ref.at[sent - near], x1b_sem.at[sent - near])
        ]
        if own < 5:
            dest = z1_refs[0].at[own] if own < first else z1_refs[1].at[own - first]
            found.append(pltpu.make_async_copy(tile, dest, z1_sem.at[own]))
        return found

    arrived = 0
    for chunk in range(CHUNKS):
        part, start = divmod(chunk * uw, wide)
        if part == arrived:
            fetches[part].wait()
            arrived += 1
        for i in range(dims.br):
            rows = slice(i * bs, (i + 1) * bs)
            mask = block_mask(pattern_ref, i, own_slots(dims, chunk, column), bs, BF16)
            kept_ref[chunk, rows, :] = tile_ref[part, rows, start : start + uw] * mask
        for lane_odd in (0, 1):

            @pl.when(odd == lane_odd)
            def _():
                for copy in copies_of(chunk, lane_odd):
                    copy.start()

    for lane_odd in (0, 1):

        @pl.when(odd == lane_odd)
        def _():
            for chunk in range(CHUNKS):
                for copy in copies_of(chunk, lane_odd):
                    copy.wait()


def own_block_cols(dims, p2_ref, slot, column):
    pair = pl.multiple_of((dims.n_col * slot // 2 + column // 2) * 2 * dims.bs, 2 * dims.bs)
    wide = p2_ref[:, pl.ds(pair, 2 * dims.bs)].astype(F32)
    return jnp.where(column % 2 == 1, wide[:, dims.bs :], wide[:, : dims.bs])


def spread_kernel(dims, *refs):
    inputs, refs = refs[:7], refs[7:]
    xt_ref, y_ref, mask_ref, wide_ref = refs[:4]
    held, sems = refs[4:11], refs[11]
    copies = [
        pltpu.make_async_copy(source, dest, sems.at[at])
        for at, (source, dest) in enumerate(zip(inputs, held))
    ]
    for copy in copies:
        copy.start()
    for copy in copies:
        copy.wait()
    pattern_ref, x_offset_ref, x_extent_ref, y_offset_ref, y_extent_ref, x_basis_ref, y_basis_ref = held
    odd = lax.axis_index("row") % 2
    column = lax.axis_index("col")
    bs, br = dims.bs, dims.br
    width = br * bs
    for i in range(br):
        for block in range(CHUNKS):
            slots = [block * br + t for t in range(br)]
            mask = block_mask(pattern_ref, i, slots, bs, F32)
            wide_ref[i : i + 1, block * width : (block + 1) * width] = mask
    tx = y_basis_ref.shape[0]
    step = lax.broadcasted_iota(jnp.int32, (tx, EY), 0)
    cell = lax.broadcasted_iota(jnp.int32, (tx, EY), 1)
    for chunk in range(CHUNKS):
        place = jnp.where(odd == 1, chunk, CHUNKS - 1 - chunk)
        for i in range(br):
            slots = own_slots(dims, chunk, column)
            mask_ref[place, i : i + 1, :] = 2.0 * block_mask(pattern_ref, i, slots, bs, F32)
        for s in range(dims.stride):
            m = chunk * dims.stride + s
            hit = (cell == y_offset_ref[0, m] + step) & (step < y_extent_ref[0, m])
            spread = lax.dot_general(
                y_basis_ref[:, m * bs : (m + 1) * bs],
                hit.astype(F32).astype(BF16),
                (((0,), (0,)), ((), ())),
                preferred_element_type=F32,
            )
            y_ref[place, s * bs : (s + 1) * bs, :] = spread.astype(BF16)
    step = lax.broadcasted_iota(jnp.int32, (EX, tx), 1)
    cell = lax.broadcasted_iota(jnp.int32, (EX, tx), 0)
    for i in range(br):
        hit = (cell == x_offset_ref[i] + step) & (step < x_extent_ref[i])
        spread = jnp.dot(
            hit.astype(F32).astype(BF16),
            x_basis_ref[:, i * bs : (i + 1) * bs],
            preferred_element_type=F32,
        )
        xt_ref[:, i * bs : (i + 1) * bs] = spread.astype(BF16)


def square_kernel(dims, p2_ref, wide_ref, *refs):
    squares_ref, summed_ref = refs[3:5]
    for source, dest in zip(refs[:3], refs[5:]):
        dest[...] = source[...]
    odd = lax.axis_index("row") % 2
    column = lax.axis_index("col")
    bs, br = dims.bs, dims.br
    width = br * bs
    for block in range(CHUNKS):
        place = jnp.where(odd == 1, block, CHUNKS - 1 - block)
        cols = slice(block * width, (block + 1) * width)
        for i in range(br):
            rows = slice(i * bs, (i + 1) * bs)
            squares_ref[place, rows, :] = p2_ref[rows, cols] * wide_ref[i : i + 1, cols].astype(BF16)
    for chunk in range(CHUNKS):
        place = jnp.where(odd == 1, chunk, CHUNKS - 1 - chunk)
        parts = [
            own_block_cols(dims, p2_ref, chunk * dims.stride + s, column)
            for s in range(dims.stride)
        ]
        own = parts[0] if len(parts) == 1 else jnp.concatenate(parts, axis=1)
        summed_ref[place] = 1.5 * own


def paired(terms):
    return [terms[at : at + 2] for at in range(0, len(terms), 2)]


def add_products(square, terms, summed_ref):
    for group in paired(terms):
        tiles = [tile[...] for _, tile in group]
        wide = tiles[0] if len(tiles) == 1 else jnp.concatenate(tiles, axis=1)
        product = jnp.dot(square, wide, preferred_element_type=F32)
        uw = tiles[0].shape[1]
        for at, (place, _) in enumerate(group):
            summed_ref[place] -= product[:, at * uw : (at + 1) * uw]


def first_kernel(squares_ref, before_ref, x1a_ref, x1b_ref, summed_ref):
    summed_ref[...] = before_ref[...]
    own = lambda j: x1a_ref.at[j] if j < NEAR else x1b_ref.at[j - NEAR]
    add_products(
        squares_ref[HD], [(k, own(CHUNKS - 1 - k)) for k in range(CHUNKS)], summed_ref
    )


def stage_kernel(terms, squares_ref, before_ref, *refs):
    summed_ref = refs[-1]
    summed_ref[...] = before_ref[...]
    for distance, pairs in terms:
        add_products(
            squares_ref[HD + distance],
            [(place, refs[which].at[at]) for place, which, at in pairs],
            summed_ref,
        )


def finish(mask_ref, k, total, new_ref, at):
    br, uw = mask_ref.shape[1:]
    bs = total.shape[0] // br
    for i in range(br):
        rows = slice(i * bs, (i + 1) * bs)
        kept = total[rows] * mask_ref[k, i : i + 1, :]
        new_ref[rows, at * uw : (at + 1) * uw] = kept.astype(BF16)


def inner_kernel(
    mask_ref, squares_ref, before_ref, x2p_ref, z3_ref, y_ref, new_ref, half_ref, edges_ref
):
    uw = edges_ref.shape[2]

    def product(distance, *tiles):
        wide = jnp.concatenate(tiles, axis=1)
        return jnp.dot(squares_ref[HD + distance], wide, preferred_element_type=F32)

    low = product(-2, x2p_ref[3], x2p_ref[2])
    mid = product(-2, x2p_ref[1], x2p_ref[0]) + product(3, z3_ref[0], z3_ref[1])
    high = product(3, z3_ref[2], z3_ref[3])
    parts = [low[:, :uw], low[:, uw:], mid[:, :uw], mid[:, uw:], high[:, :uw]]
    for at, part in enumerate(parts):
        finish(mask_ref, at + 1, before_ref[at + 1] - part, new_ref, at)
    edges_ref[0] = before_ref[0]
    edges_ref[1] = before_ref[CHUNKS - 1] - high[:, uw:]
    inner = y_ref[1 : CHUNKS - 1].reshape((CHUNKS - 2) * uw, EY)
    half_ref[...] = jnp.dot(new_ref[...], inner, preferred_element_type=F32)


def last_kernel(
    mask_ref,
    squares_ref,
    edges_ref,
    x2q_ref,
    z1b_ref,
    xt_ref,
    y_ref,
    half_ref,
    new_ref,
    middle_ref,
    rim_a_ref,
    rim_b_ref,
):
    odd = lax.axis_index("row") % 2
    product = lambda d, tile: jnp.dot(squares_ref[HD + d], tile, preferred_element_type=F32)
    finish(mask_ref, 0, edges_ref[0] - product(-2, x2q_ref[0]), new_ref, 0)
    finish(mask_ref, CHUNKS - 1, edges_ref[1] - product(2, z1b_ref[0]), new_ref, 1)
    outer = jnp.concatenate([y_ref[0], y_ref[CHUNKS - 1]], axis=0)
    half = half_ref[...] + jnp.dot(new_ref[...], outer, preferred_element_type=F32)
    extended = jnp.dot(xt_ref[...], half.astype(BF16), preferred_element_type=F32)
    middle_ref[...] = extended[M : M + SX]
    lower, upper = extended[:M], extended[SX + M :]
    rim_a_ref[...] = jnp.where(odd == 1, lower, upper).astype(BF16)
    rim_b_ref[...] = jnp.where(odd == 1, upper, lower).astype(BF16)


def order_kernel(inner_ref, edges_ref, new_ref):
    odd = lax.axis_index("row") % 2
    uw = edges_ref.shape[1] // 2

    @pl.when(odd == 1)
    def _():
        new_ref[:, :uw] = edges_ref[:, :uw]
        new_ref[:, uw : (CHUNKS - 1) * uw] = inner_ref[...]
        new_ref[:, (CHUNKS - 1) * uw :] = edges_ref[:, uw:]

    @pl.when(odd == 0)
    def _():
        new_ref[:, :uw] = edges_ref[:, uw:]
        for at in range(CHUNKS - 2):
            place = CHUNKS - 2 - at
            new_ref[:, place * uw : (place + 1) * uw] = inner_ref[:, at * uw : (at + 1) * uw]
        new_ref[:, (CHUNKS - 1) * uw :] = edges_ref[:, :uw]


def row_rims_kernel(middle_ref, got_a_ref, got_b_ref, center_ref, rim_a_ref, rim_b_ref):
    odd = lax.axis_index("row") % 2
    col_odd = lax.axis_index("col") % 2
    got_a, got_b = got_a_ref[...].astype(F32), got_b_ref[...].astype(F32)
    low = jnp.where(odd == 1, got_a, got_b)
    high = jnp.where(odd == 1, got_b, got_a)
    interior = jnp.concatenate(
        [middle_ref[:M] + low, middle_ref[M : SX - M], middle_ref[SX - M :] + high], axis=0
    )
    center_ref[...] = interior[:, M : M + SY]
    lower = interior[:, :SY].T[:M]
    upper = interior[:, EY - SY :].T[SY - M :]
    rim_a_ref[...] = jnp.where(col_odd == 1, lower, upper).astype(BF16)
    rim_b_ref[...] = jnp.where(col_odd == 1, upper, lower).astype(BF16)


def col_rims_kernel(center_ref, got_a_ref, got_b_ref, grid_ref):
    col_odd = lax.axis_index("col") % 2
    got_a, got_b = got_a_ref[...].astype(F32), got_b_ref[...].astype(F32)
    low = jnp.where(col_odd == 1, got_a, got_b)
    high = jnp.where(col_odd == 1, got_b, got_a)
    none = jnp.zeros((SY - 2 * M, SX), F32)
    grid_ref[...] = center_ref[...] + jnp.concatenate([low, none, high], axis=0).T


def swap_partner(value, axis):
    count = lax.axis_size(axis)
    return lax.ppermute(value, axis, [(s, s ^ 1) for s in range(count)])


def swap_other(value, axis):
    count = lax.axis_size(axis)
    pairs = [(s, (s - 1) % count if s % 2 == 0 else (s + 1) % count) for s in range(count)]
    return lax.ppermute(value, axis, pairs)


def shift_level(value):
    count = lax.axis_size("row")
    pairs = [(s, (s + 2) % count if s % 2 == 0 else (s - 2) % count) for s in range(count)]
    return lax.ppermute(value, "row", pairs)


def after(value, *others):
    return lax.optimization_barrier((value,) + others)[0]


def call(kernel, outs, ins, scratch=(), beside=0, stay=(), outs_stay=False, limit=24):
    shapes = [jax.ShapeDtypeStruct(shape, dtype) for shape, dtype in outs]
    specs = [
        HBM
        if at in stay
        else SMEM
        if jnp.issubdtype(value.dtype, jnp.integer)
        else VMEM
        for at, value in enumerate(ins)
    ]
    moved = sum(value.size * value.dtype.itemsize for value in list(ins) + shapes)
    return pl.pallas_call(
        kernel,
        out_shape=shapes,
        in_specs=specs,
        out_specs=[HBM if outs_stay else VMEM] * len(shapes),
        scratch_shapes=list(scratch),
        compiler_params=pltpu.CompilerParams(vmem_limit_bytes=limit * 2**20),
        cost_estimate=pl.CostEstimate(
            flops=beside * 10**9, bytes_accessed=moved, transcendentals=0
        ),
    )(*ins)


def shards(p2_panel, density, pattern, x_basis, x_offset, x_extent, y_basis, y_offset, y_extent):
    dims = Dims(pattern, x_basis, lax.axis_size("col"))
    rows, uw = dims.rows, dims.uw
    chunks = lambda count: ((count, rows, uw), BF16)
    total = ((CHUNKS, rows, uw), F32)

    parts = CHUNKS if uw % 128 == 0 else 1
    own_p, own_q, own_z, own_zb = call(
        functools.partial(mask_kernel, dims),
        [chunks(NEAR), chunks(CHUNKS - NEAR), chunks(NEAR), chunks(AHEAD - NEAR)],
        [pattern, density],
        scratch=[
            pltpu.SMEM(pattern.shape, jnp.int32),
            pltpu.VMEM((parts, rows, CHUNKS * uw // parts), BF16),
            pltpu.VMEM((CHUNKS, rows, uw), BF16),
            pltpu.SemaphoreType.DMA(()),
            pltpu.SemaphoreType.DMA((parts,)),
            pltpu.SemaphoreType.DMA((NEAR,)),
            pltpu.SemaphoreType.DMA((CHUNKS - NEAR,)),
            pltpu.SemaphoreType.DMA((AHEAD,)),
        ],
        stay=(0, 1),
        outs_stay=True,
        limit=60,
    )
    x1p = swap_partner(own_p, "row")
    z1 = shift_level(own_z)
    x1q = swap_partner(own_q, "row")

    small = [pattern, x_offset, x_extent, y_offset, y_extent, x_basis.T, y_basis[0].T]
    xt, y_spread, mask, wide = call(
        functools.partial(spread_kernel, dims),
        [
            ((EX, rows), BF16),
            ((CHUNKS, uw, EY), BF16),
            ((CHUNKS, dims.br, uw), F32),
            ((dims.br, dims.win * dims.bs), F32),
        ],
        small,
        scratch=[
            (pltpu.SMEM if jnp.issubdtype(value.dtype, jnp.integer) else pltpu.VMEM)(
                value.shape, value.dtype
            )
            for value in small
        ]
        + [pltpu.SemaphoreType.DMA((len(small),))],
        stay=range(len(small)),
        limit=60,
        beside=6,
    )
    kept = [xt, y_spread, mask]
    squares, summed, xt, y_spread, mask = call(
        functools.partial(square_kernel, dims),
        [((CHUNKS, rows, rows), BF16), total] + [(value.shape, value.dtype) for value in kept],
        [p2_panel, wide] + kept,
        beside=1,
    )
    ready = summed

    def stage(summed, terms, beside=0):
        tiles = []
        for _, pairs in terms:
            for _, tile, _ in pairs:
                if not any(tile is known for known in tiles):
                    tiles.append(tile)
        spot = lambda tile: next(at for at, known in enumerate(tiles) if known is tile)
        listed = [(d, [(place, spot(tile), at) for place, tile, at in pairs]) for d, pairs in terms]
        return call(
            functools.partial(stage_kernel, listed),
            [total],
            [squares, summed] + tiles,
            beside=beside,
        )[0]

    (summed,) = call(first_kernel, [total], [squares, summed, own_p, own_q])
    z2p = shift_level(after(x1p, ready))
    x3 = swap_partner(z1, "row")
    z2q = shift_level(x1q[: 2 * HD - NEAR])
    z1b = shift_level(after(own_zb, z1))
    partner = [(j - 1, x1p, j) for j in range(1, NEAR)]
    partner += [(j - 1, x1q, j - NEAR) for j in range(NEAR, CHUNKS)]
    summed = stage(
        summed, [(-1, partner), (2, [(j + 2, z1, j) for j in range(NEAR)])], beside=3
    )
    x2p = swap_partner(after(z2p, summed), "row")
    z3 = shift_level(z2p)
    summed = stage(summed, [(1, [(j + 1, z2p, j) for j in range(NEAR)])])
    x2q = swap_partner(after(z2q[: AHEAD - NEAR], z2p), "row")
    summed = stage(
        summed,
        [
            (1, [(j + 1, z2q, j - NEAR) for j in range(NEAR, 2 * HD)]),
            (-3, [(3 - j, x3, j) for j in range(NEAR)]),
        ],
        beside=4,
    )
    new_inner, half, edges = call(
        inner_kernel,
        [((rows, (CHUNKS - 2) * uw), BF16), ((rows, EY), F32), ((2, rows, uw), F32)],
        [mask, squares, summed, x2p, z3, y_spread],
        beside=0,
    )
    new_edges, middle, rim_a, rim_b = call(
        last_kernel,
        [((rows, 2 * uw), BF16), ((SX, EY), F32), ((M, EY), BF16), ((M, EY), BF16)],
        [mask, squares, edges, x2q, z1b, xt, y_spread, half],
    )
    (new_density,) = call(
        order_kernel, [((rows, dims.wc * dims.bs), BF16)], [new_inner, new_edges]
    )
    got_a = swap_partner(rim_a, "row")
    got_b = swap_other(rim_b, "row")
    center, rim_a, rim_b = call(
        row_rims_kernel,
        [((SX, SY), F32), ((M, SX), BF16), ((M, SX), BF16)],
        [after(middle, new_density), got_a, got_b],
    )
    got_a = swap_partner(rim_a, "col")
    got_b = swap_other(rim_b, "col")
    (grid_density,) = call(col_rims_kernel, [((SX, SY), F32)], [center, got_a, got_b])
    return new_density, grid_density


def solution(mesh):
    placed = (
        P("row", None),
        P("row", "col"),
        P("row", None),
        P("row", None),
        P("row"),
        P("row"),
        P("row", "col", None),
        P("row", "col"),
        P("row", "col"),
    )
    return jax.shard_map(
        shards,
        mesh=mesh,
        in_specs=placed,
        out_specs=(P("row", "col"), P("row", "col")),
        check_vma=False,
    )
```

```python
import functools

import jax
import jax.numpy as jnp
from jax import lax
from jax.experimental import pallas as pl
from jax.experimental.pallas import tpu as pltpu
from jax.sharding import PartitionSpec as P

HD = 3
SX = 128
SY = 128
M = 32
EX = SX + 2 * M
EY = SY + 2 * M
CHUNKS = 2 * HD + 1
NEAR = HD + 1
AHEAD = HD + 2
VMEM = pl.BlockSpec(memory_space=pltpu.VMEM)
SMEM = pl.BlockSpec(memory_space=pltpu.SMEM)
HBM = pl.BlockSpec(memory_space=pltpu.HBM)
F32 = jnp.float32
BF16 = jnp.bfloat16


class Dims:
    def __init__(self, pattern, x_basis, n_col):
        self.br, self.win = pattern.shape
        self.bs = x_basis.shape[0] // self.br
        self.n_col = n_col
        self.wc = self.win // n_col
        self.stride = self.br // n_col
        self.uw = self.stride * self.bs
        self.rows = self.br * self.bs


def block_mask(pattern_ref, block_row, slots, bs, dtype):
    lane = lax.broadcasted_iota(jnp.int32, (1, bs * len(slots)), 1)
    row = jnp.zeros((1, bs * len(slots)), jnp.int32)
    for place, slot in enumerate(slots):
        inside = (lane >= place * bs) & (lane < (place + 1) * bs)
        row = jnp.where(inside, pattern_ref[block_row, slot], row)
    return row.astype(F32).astype(dtype)


def own_slots(dims, chunk, column):
    return [dims.n_col * (chunk * dims.stride + s) + column for s in range(dims.stride)]


def mask_kernel(
    dims,
    pattern_hbm,
    density_hbm,
    x1a_ref,
    x1b_ref,
    *refs,
):
    z1_refs, refs = refs[:-8], refs[-8:]
    pattern_ref, tile_ref, kept_ref, pattern_sem, tile_sems, x1a_sem, x1b_sem, z1_sem = refs
    odd = lax.axis_index("row") % 2
    column = lax.axis_index("col")
    bs, uw = dims.bs, dims.uw
    wide = tile_ref.shape[2]
    fetch_pattern = pltpu.make_async_copy(pattern_hbm, pattern_ref, pattern_sem)
    fetch_pattern.start()
    fetches = []
    for part in range(tile_ref.shape[0]):
        cols = pl.ds(part * wide, wide)
        fetch = pltpu.make_async_copy(density_hbm.at[:, cols], tile_ref.at[part], tile_sems.at[part])
        fetch.start()
        fetches.append(fetch)
    fetch_pattern.wait()
    near, first = x1a_ref.shape[0], z1_refs[0].shape[0]

    def copies_of(chunk, lane_odd):
        own = chunk if lane_odd else CHUNKS - 1 - chunk
        sent = CHUNKS - 1 - own
        tile = kept_ref.at[chunk]
        found = [
            pltpu.make_async_copy(tile, x1a_ref.at[sent], x1a_sem.at[sent])
            if sent < near
            else pltpu.make_async_copy(tile, x1b_ref.at[sent - near], x1b_sem.at[sent - near])
        ]
        if own < 5:
            dest = z1_refs[0].at[own] if own < first else z1_refs[1].at[own - first]
            found.append(pltpu.make_async_copy(tile, dest, z1_sem.at[own]))
        return found

    arrived = 0
    for chunk in range(CHUNKS):
        part, start = divmod(chunk * uw, wide)
        if part == arrived:
            fetches[part].wait()
            arrived += 1
        for i in range(dims.br):
            rows = slice(i * bs, (i + 1) * bs)
            mask = block_mask(pattern_ref, i, own_slots(dims, chunk, column), bs, BF16)
            kept_ref[chunk, rows, :] = tile_ref[part, rows, start : start + uw] * mask
        for lane_odd in (0, 1):

            @pl.when(odd == lane_odd)
            def _():
                for copy in copies_of(chunk, lane_odd):
                    copy.start()

    for lane_odd in (0, 1):

        @pl.when(odd == lane_odd)
        def _():
            for chunk in range(CHUNKS):
                for copy in copies_of(chunk, lane_odd):
                    copy.wait()


def own_block_cols(dims, p2_ref, slot, column):
    pair = pl.multiple_of((dims.n_col * slot // 2 + column // 2) * 2 * dims.bs, 2 * dims.bs)
    wide = p2_ref[:, pl.ds(pair, 2 * dims.bs)].astype(F32)
    return jnp.where(column % 2 == 1, wide[:, dims.bs :], wide[:, : dims.bs])


def spread_kernel(dims, *refs):
    inputs, refs = refs[:7], refs[7:]
    xt_ref, y_ref, mask_ref, wide_ref = refs[:4]
    held, sems = refs[4:11], refs[11]
    copies = [
        pltpu.make_async_copy(source, dest, sems.at[at])
        for at, (source, dest) in enumerate(zip(inputs, held))
    ]
    for copy in copies:
        copy.start()
    for copy in copies:
        copy.wait()
    pattern_ref, x_offset_ref, x_extent_ref, y_offset_ref, y_extent_ref, x_basis_ref, y_basis_ref = held
    odd = lax.axis_index("row") % 2
    column = lax.axis_index("col")
    bs, br = dims.bs, dims.br
    width = br * bs
    for i in range(br):
        for block in range(CHUNKS):
            slots = [block * br + t for t in range(br)]
            mask = block_mask(pattern_ref, i, slots, bs, F32)
            wide_ref[i : i + 1, block * width : (block + 1) * width] = mask
    tx = y_basis_ref.shape[0]
    step = lax.broadcasted_iota(jnp.int32, (tx, EY), 0)
    cell = lax.broadcasted_iota(jnp.int32, (tx, EY), 1)
    for chunk in range(CHUNKS):
        place = jnp.where(odd == 1, chunk, CHUNKS - 1 - chunk)
        for i in range(br):
            slots = own_slots(dims, chunk, column)
            mask_ref[place, i : i + 1, :] = 2.0 * block_mask(pattern_ref, i, slots, bs, F32)
        for s in range(dims.stride):
            m = chunk * dims.stride + s
            hit = (cell == y_offset_ref[0, m] + step) & (step < y_extent_ref[0, m])
            spread = lax.dot_general(
                y_basis_ref[:, m * bs : (m + 1) * bs],
                hit.astype(F32).astype(BF16),
                (((0,), (0,)), ((), ())),
                preferred_element_type=F32,
            )
            y_ref[place, s * bs : (s + 1) * bs, :] = spread.astype(BF16)
    step = lax.broadcasted_iota(jnp.int32, (EX, tx), 1)
    cell = lax.broadcasted_iota(jnp.int32, (EX, tx), 0)
    for i in range(br):
        hit = (cell == x_offset_ref[i] + step) & (step < x_extent_ref[i])
        spread = jnp.dot(
            hit.astype(F32).astype(BF16),
            x_basis_ref[:, i * bs : (i + 1) * bs],
            preferred_element_type=F32,
        )
        xt_ref[:, i * bs : (i + 1) * bs] = spread.astype(BF16)


def square_kernel(dims, p2_ref, wide_ref, *refs):
    squares_ref, summed_ref = refs[3:5]
    for source, dest in zip(refs[:3], refs[5:]):
        dest[...] = source[...]
    odd = lax.axis_index("row") % 2
    column = lax.axis_index("col")
    bs, br = dims.bs, dims.br
    width = br * bs
    for block in range(CHUNKS):
        place = jnp.where(odd == 1, block, CHUNKS - 1 - block)
        cols = slice(block * width, (block + 1) * width)
        for i in range(br):
            rows = slice(i * bs, (i + 1) * bs)
            squares_ref[place, rows, :] = p2_ref[rows, cols] * wide_ref[i : i + 1, cols].astype(BF16)
    for chunk in range(CHUNKS):
        place = jnp.where(odd == 1, chunk, CHUNKS - 1 - chunk)
        parts = [
            own_block_cols(dims, p2_ref, chunk * dims.stride + s, column)
            for s in range(dims.stride)
        ]
        own = parts[0] if len(parts) == 1 else jnp.concatenate(parts, axis=1)
        summed_ref[place] = 1.5 * own


def paired(terms):
    return [terms[at : at + 2] for at in range(0, len(terms), 2)]


def add_products(square, terms, summed_ref):
    for group in paired(terms):
        tiles = [tile[...] for _, tile in group]
        wide = tiles[0] if len(tiles) == 1 else jnp.concatenate(tiles, axis=1)
        product = jnp.dot(square, wide, preferred_element_type=F32)
        uw = tiles[0].shape[1]
        for at, (place, _) in enumerate(group):
            summed_ref[place] -= product[:, at * uw : (at + 1) * uw]


def first_kernel(squares_ref, before_ref, x1a_ref, x1b_ref, summed_ref):
    summed_ref[...] = before_ref[...]
    own = lambda j: x1a_ref.at[j] if j < NEAR else x1b_ref.at[j - NEAR]
    add_products(
        squares_ref[HD], [(k, own(CHUNKS - 1 - k)) for k in range(CHUNKS)], summed_ref
    )


def stage_kernel(terms, squares_ref, before_ref, *refs):
    summed_ref = refs[-1]
    summed_ref[...] = before_ref[...]
    for distance, pairs in terms:
        add_products(
            squares_ref[HD + distance],
            [(place, refs[which].at[at]) for place, which, at in pairs],
            summed_ref,
        )


def finish(mask_ref, k, total, new_ref, at):
    br, uw = mask_ref.shape[1:]
    bs = total.shape[0] // br
    for i in range(br):
        rows = slice(i * bs, (i + 1) * bs)
        kept = total[rows] * mask_ref[k, i : i + 1, :]
        new_ref[rows, at * uw : (at + 1) * uw] = kept.astype(BF16)


def inner_kernel(
    mask_ref, squares_ref, before_ref, x2p_ref, z3_ref, y_ref, new_ref, half_ref, edges_ref
):
    uw = edges_ref.shape[2]

    def product(distance, *tiles):
        wide = jnp.concatenate(tiles, axis=1)
        return jnp.dot(squares_ref[HD + distance], wide, preferred_element_type=F32)

    low = product(-2, x2p_ref[3], x2p_ref[2])
    mid = product(-2, x2p_ref[1], x2p_ref[0]) + product(3, z3_ref[0], z3_ref[1])
    high = product(3, z3_ref[2], z3_ref[3])
    parts = [low[:, :uw], low[:, uw:], mid[:, :uw], mid[:, uw:], high[:, :uw]]
    for at, part in enumerate(parts):
        finish(mask_ref, at + 1, before_ref[at + 1] - part, new_ref, at)
    edges_ref[0] = before_ref[0]
    edges_ref[1] = before_ref[CHUNKS - 1] - high[:, uw:]
    inner = y_ref[1 : CHUNKS - 1].reshape((CHUNKS - 2) * uw, EY)
    half_ref[...] = jnp.dot(new_ref[...], inner, preferred_element_type=F32)


def last_kernel(
    mask_ref,
    squares_ref,
    edges_ref,
    x2q_ref,
    z1b_ref,
    xt_ref,
    y_ref,
    half_ref,
    new_ref,
    middle_ref,
    rim_a_ref,
    rim_b_ref,
):
    odd = lax.axis_index("row") % 2
    product = lambda d, tile: jnp.dot(squares_ref[HD + d], tile, preferred_element_type=F32)
    finish(mask_ref, 0, edges_ref[0] - product(-2, x2q_ref[0]), new_ref, 0)
    finish(mask_ref, CHUNKS - 1, edges_ref[1] - product(2, z1b_ref[0]), new_ref, 1)
    outer = jnp.concatenate([y_ref[0], y_ref[CHUNKS - 1]], axis=0)
    half = half_ref[...] + jnp.dot(new_ref[...], outer, preferred_element_type=F32)
    extended = jnp.dot(xt_ref[...], half.astype(BF16), preferred_element_type=F32)
    middle_ref[...] = extended[M : M + SX]
    lower, upper = extended[:M], extended[SX + M :]
    rim_a_ref[...] = jnp.where(odd == 1, lower, upper).astype(BF16)
    rim_b_ref[...] = jnp.where(odd == 1, upper, lower).astype(BF16)


def order_kernel(inner_ref, edges_ref, new_ref):
    odd = lax.axis_index("row") % 2
    uw = edges_ref.shape[1] // 2

    @pl.when(odd == 1)
    def _():
        new_ref[:, :uw] = edges_ref[:, :uw]
        new_ref[:, uw : (CHUNKS - 1) * uw] = inner_ref[...]
        new_ref[:, (CHUNKS - 1) * uw :] = edges_ref[:, uw:]

    @pl.when(odd == 0)
    def _():
        new_ref[:, :uw] = edges_ref[:, uw:]
        for at in range(CHUNKS - 2):
            place = CHUNKS - 2 - at
            new_ref[:, place * uw : (place + 1) * uw] = inner_ref[:, at * uw : (at + 1) * uw]
        new_ref[:, (CHUNKS - 1) * uw :] = edges_ref[:, :uw]


def row_rims_kernel(middle_ref, got_a_ref, got_b_ref, center_ref, rim_a_ref, rim_b_ref):
    odd = lax.axis_index("row") % 2
    col_odd = lax.axis_index("col") % 2
    got_a, got_b = got_a_ref[...].astype(F32), got_b_ref[...].astype(F32)
    low = jnp.where(odd == 1, got_a, got_b)
    high = jnp.where(odd == 1, got_b, got_a)
    interior = jnp.concatenate(
        [middle_ref[:M] + low, middle_ref[M : SX - M], middle_ref[SX - M :] + high], axis=0
    )
    center_ref[...] = interior[:, M : M + SY]
    lower = interior[:, :SY].T[:M]
    upper = interior[:, EY - SY :].T[SY - M :]
    rim_a_ref[...] = jnp.where(col_odd == 1, lower, upper).astype(BF16)
    rim_b_ref[...] = jnp.where(col_odd == 1, upper, lower).astype(BF16)


def col_rims_kernel(center_ref, got_a_ref, got_b_ref, grid_ref):
    col_odd = lax.axis_index("col") % 2
    got_a, got_b = got_a_ref[...].astype(F32), got_b_ref[...].astype(F32)
    low = jnp.where(col_odd == 1, got_a, got_b)
    high = jnp.where(col_odd == 1, got_b, got_a)
    none = jnp.zeros((SY - 2 * M, SX), F32)
    grid_ref[...] = center_ref[...] + jnp.concatenate([low, none, high], axis=0).T


def swap_partner(value, axis):
    count = lax.axis_size(axis)
    return lax.ppermute(value, axis, [(s, s ^ 1) for s in range(count)])


def swap_other(value, axis):
    count = lax.axis_size(axis)
    pairs = [(s, (s - 1) % count if s % 2 == 0 else (s + 1) % count) for s in range(count)]
    return lax.ppermute(value, axis, pairs)


def shift_level(value):
    count = lax.axis_size("row")
    pairs = [(s, (s + 2) % count if s % 2 == 0 else (s - 2) % count) for s in range(count)]
    return lax.ppermute(value, "row", pairs)


def after(value, *others):
    return lax.optimization_barrier((value,) + others)[0]


def call(kernel, outs, ins, scratch=(), beside=0, stay=(), outs_stay=False, limit=24):
    shapes = [jax.ShapeDtypeStruct(shape, dtype) for shape, dtype in outs]
    specs = [
        HBM
        if at in stay
        else SMEM
        if jnp.issubdtype(value.dtype, jnp.integer)
        else VMEM
        for at, value in enumerate(ins)
    ]
    moved = sum(value.size * value.dtype.itemsize for value in list(ins) + shapes)
    return pl.pallas_call(
        kernel,
        out_shape=shapes,
        in_specs=specs,
        out_specs=[HBM if outs_stay else VMEM] * len(shapes),
        scratch_shapes=list(scratch),
        compiler_params=pltpu.CompilerParams(vmem_limit_bytes=limit * 2**20),
        cost_estimate=pl.CostEstimate(
            flops=beside * 10**9, bytes_accessed=moved, transcendentals=0
        ),
    )(*ins)


def shards(p2_panel, density, pattern, x_basis, x_offset, x_extent, y_basis, y_offset, y_extent):
    dims = Dims(pattern, x_basis, lax.axis_size("col"))
    rows, uw = dims.rows, dims.uw
    chunks = lambda count: ((count, rows, uw), BF16)
    total = ((CHUNKS, rows, uw), F32)

    parts = CHUNKS if uw % 128 == 0 else 1
    own_p, own_q, own_z, own_zb = call(
        functools.partial(mask_kernel, dims),
        [chunks(NEAR), chunks(CHUNKS - NEAR), chunks(NEAR), chunks(AHEAD - NEAR)],
        [pattern, density],
        scratch=[
            pltpu.SMEM(pattern.shape, jnp.int32),
            pltpu.VMEM((parts, rows, CHUNKS * uw // parts), BF16),
            pltpu.VMEM((CHUNKS, rows, uw), BF16),
            pltpu.SemaphoreType.DMA(()),
            pltpu.SemaphoreType.DMA((parts,)),
            pltpu.SemaphoreType.DMA((NEAR,)),
            pltpu.SemaphoreType.DMA((CHUNKS - NEAR,)),
            pltpu.SemaphoreType.DMA((AHEAD,)),
        ],
        stay=(0, 1),
        outs_stay=True,
        limit=60,
    )
    x1p = swap_partner(own_p, "row")
    z1 = shift_level(own_z)
    x1q = swap_partner(own_q, "row")

    small = [pattern, x_offset, x_extent, y_offset, y_extent, x_basis.T, y_basis[0].T]
    xt, y_spread, mask, wide = call(
        functools.partial(spread_kernel, dims),
        [
            ((EX, rows), BF16),
            ((CHUNKS, uw, EY), BF16),
            ((CHUNKS, dims.br, uw), F32),
            ((dims.br, dims.win * dims.bs), F32),
        ],
        small,
        scratch=[
            (pltpu.SMEM if jnp.issubdtype(value.dtype, jnp.integer) else pltpu.VMEM)(
                value.shape, value.dtype
            )
            for value in small
        ]
        + [pltpu.SemaphoreType.DMA((len(small),))],
        stay=range(len(small)),
        limit=60,
        beside=6,
    )
    kept = [xt, y_spread, mask]
    squares, summed, xt, y_spread, mask = call(
        functools.partial(square_kernel, dims),
        [((CHUNKS, rows, rows), BF16), total] + [(value.shape, value.dtype) for value in kept],
        [p2_panel, wide] + kept,
        beside=1,
    )
    ready = summed

    def stage(summed, terms, beside=0):
        tiles = []
        for _, pairs in terms:
            for _, tile, _ in pairs:
                if not any(tile is known for known in tiles):
                    tiles.append(tile)
        spot = lambda tile: next(at for at, known in enumerate(tiles) if known is tile)
        listed = [(d, [(place, spot(tile), at) for place, tile, at in pairs]) for d, pairs in terms]
        return call(
            functools.partial(stage_kernel, listed),
            [total],
            [squares, summed] + tiles,
            beside=beside,
        )[0]

    (summed,) = call(first_kernel, [total], [squares, summed, own_p, own_q])
    z2p = shift_level(after(x1p, ready))
    x3 = swap_partner(z1, "row")
    z2q = shift_level(x1q[: 2 * HD - NEAR])
    z1b = shift_level(after(own_zb, z1))
    partner = [(j - 1, x1p, j) for j in range(1, NEAR)]
    partner += [(j - 1, x1q, j - NEAR) for j in range(NEAR, CHUNKS)]
    summed = stage(
        summed, [(-1, partner), (2, [(j + 2, z1, j) for j in range(NEAR)])], beside=3
    )
    x2p = swap_partner(after(z2p, summed), "row")
    z3 = shift_level(z2p)
    summed = stage(summed, [(1, [(j + 1, z2p, j) for j in range(NEAR)])])
    x2q = swap_partner(z2q[: AHEAD - NEAR], "row")
    summed = stage(
        summed,
        [
            (1, [(j + 1, z2q, j - NEAR) for j in range(NEAR, 2 * HD)]),
            (-3, [(3 - j, x3, j) for j in range(NEAR)]),
        ],
        beside=4,
    )
    new_inner, half, edges = call(
        inner_kernel,
        [((rows, (CHUNKS - 2) * uw), BF16), ((rows, EY), F32), ((2, rows, uw), F32)],
        [mask, squares, summed, x2p, z3, y_spread],
        beside=0,
    )
    new_edges, middle, rim_a, rim_b = call(
        last_kernel,
        [((rows, 2 * uw), BF16), ((SX, EY), F32), ((M, EY), BF16), ((M, EY), BF16)],
        [mask, squares, edges, x2q, z1b, xt, y_spread, half],
    )
    (new_density,) = call(
        order_kernel, [((rows, dims.wc * dims.bs), BF16)], [new_inner, new_edges]
    )
    got_a = swap_partner(rim_a, "row")
    got_b = swap_other(rim_b, "row")
    center, rim_a, rim_b = call(
        row_rims_kernel,
        [((SX, SY), F32), ((M, SX), BF16), ((M, SX), BF16)],
        [after(middle, new_density), got_a, got_b],
    )
    got_a = swap_partner(rim_a, "col")
    got_b = swap_other(rim_b, "col")
    (grid_density,) = call(col_rims_kernel, [((SX, SY), F32)], [center, got_a, got_b])
    return new_density, grid_density


def solution(mesh):
    placed = (
        P("row", None),
        P("row", "col"),
        P("row", None),
        P("row", None),
        P("row"),
        P("row"),
        P("row", "col", None),
        P("row", "col"),
        P("row", "col"),
    )
    return jax.shard_map(
        shards,
        mesh=mesh,
        in_specs=placed,
        out_specs=(P("row", "col"), P("row", "col")),
        check_vma=False,
    )
```

```python
import functools

import jax
import jax.numpy as jnp
from jax import lax
from jax.experimental import pallas as pl
from jax.experimental.pallas import tpu as pltpu
from jax.sharding import PartitionSpec as P

HD = 3
SX = 128
SY = 128
M = 32
EX = SX + 2 * M
EY = SY + 2 * M
CHUNKS = 2 * HD + 1
NEAR = HD + 1
AHEAD = HD + 2
VMEM = pl.BlockSpec(memory_space=pltpu.VMEM)
SMEM = pl.BlockSpec(memory_space=pltpu.SMEM)
HBM = pl.BlockSpec(memory_space=pltpu.HBM)
F32 = jnp.float32
BF16 = jnp.bfloat16


class Dims:
    def __init__(self, pattern, x_basis, n_col):
        self.br, self.win = pattern.shape
        self.bs = x_basis.shape[0] // self.br
        self.n_col = n_col
        self.wc = self.win // n_col
        self.stride = self.br // n_col
        self.uw = self.stride * self.bs
        self.rows = self.br * self.bs


def block_mask(pattern_ref, block_row, slots, bs, dtype):
    lane = lax.broadcasted_iota(jnp.int32, (1, bs * len(slots)), 1)
    row = jnp.zeros((1, bs * len(slots)), jnp.int32)
    for place, slot in enumerate(slots):
        inside = (lane >= place * bs) & (lane < (place + 1) * bs)
        row = jnp.where(inside, pattern_ref[block_row, slot], row)
    return row.astype(F32).astype(dtype)


def own_slots(dims, chunk, column):
    return [dims.n_col * (chunk * dims.stride + s) + column for s in range(dims.stride)]


def mask_kernel(
    dims,
    pattern_hbm,
    density_hbm,
    x1a_ref,
    x1b_ref,
    *refs,
):
    z1_refs, refs = refs[:-8], refs[-8:]
    pattern_ref, tile_ref, kept_ref, pattern_sem, tile_sems, x1a_sem, x1b_sem, z1_sem = refs
    odd = lax.axis_index("row") % 2
    column = lax.axis_index("col")
    bs, uw = dims.bs, dims.uw
    wide = tile_ref.shape[2]
    fetch_pattern = pltpu.make_async_copy(pattern_hbm, pattern_ref, pattern_sem)
    fetch_pattern.start()
    fetches = []
    for part in range(tile_ref.shape[0]):
        cols = pl.ds(part * wide, wide)
        fetch = pltpu.make_async_copy(density_hbm.at[:, cols], tile_ref.at[part], tile_sems.at[part])
        fetch.start()
        fetches.append(fetch)
    fetch_pattern.wait()
    near, first = x1a_ref.shape[0], z1_refs[0].shape[0]

    def copies_of(chunk, lane_odd):
        own = chunk if lane_odd else CHUNKS - 1 - chunk
        sent = CHUNKS - 1 - own
        tile = kept_ref.at[chunk]
        found = [
            pltpu.make_async_copy(tile, x1a_ref.at[sent], x1a_sem.at[sent])
            if sent < near
            else pltpu.make_async_copy(tile, x1b_ref.at[sent - near], x1b_sem.at[sent - near])
        ]
        if own < 5:
            dest = z1_refs[0].at[own] if own < first else z1_refs[1].at[own - first]
            found.append(pltpu.make_async_copy(tile, dest, z1_sem.at[own]))
        return found

    arrived = 0
    for chunk in range(CHUNKS):
        part, start = divmod(chunk * uw, wide)
        if part == arrived:
            fetches[part].wait()
            arrived += 1
        for i in range(dims.br):
            rows = slice(i * bs, (i + 1) * bs)
            mask = block_mask(pattern_ref, i, own_slots(dims, chunk, column), bs, BF16)
            kept_ref[chunk, rows, :] = tile_ref[part, rows, start : start + uw] * mask
        for lane_odd in (0, 1):

            @pl.when(odd == lane_odd)
            def _():
                for copy in copies_of(chunk, lane_odd):
                    copy.start()

    for lane_odd in (0, 1):

        @pl.when(odd == lane_odd)
        def _():
            for chunk in range(CHUNKS):
                for copy in copies_of(chunk, lane_odd):
                    copy.wait()


def own_block_cols(dims, p2_ref, slot, column):
    pair = pl.multiple_of((dims.n_col * slot // 2 + column // 2) * 2 * dims.bs, 2 * dims.bs)
    wide = p2_ref[:, pl.ds(pair, 2 * dims.bs)].astype(F32)
    return jnp.where(column % 2 == 1, wide[:, dims.bs :], wide[:, : dims.bs])


def spread_kernel(dims, *refs):
    inputs, refs = refs[:7], refs[7:]
    xt_ref, y_ref, mask_ref, wide_ref = refs[:4]
    held, sems = refs[4:11], refs[11]
    copies = [
        pltpu.make_async_copy(source, dest, sems.at[at])
        for at, (source, dest) in enumerate(zip(inputs, held))
    ]
    for copy in copies:
        copy.start()
    for copy in copies:
        copy.wait()
    pattern_ref, x_offset_ref, x_extent_ref, y_offset_ref, y_extent_ref, x_basis_ref, y_basis_ref = held
    odd = lax.axis_index("row") % 2
    column = lax.axis_index("col")
    bs, br = dims.bs, dims.br
    width = br * bs
    for i in range(br):
        for block in range(CHUNKS):
            slots = [block * br + t for t in range(br)]
            mask = block_mask(pattern_ref, i, slots, bs, F32)
            wide_ref[i : i + 1, block * width : (block + 1) * width] = mask
    tx = y_basis_ref.shape[0]
    step = lax.broadcasted_iota(jnp.int32, (tx, EY), 0)
    cell = lax.broadcasted_iota(jnp.int32, (tx, EY), 1)
    for chunk in range(CHUNKS):
        place = jnp.where(odd == 1, chunk, CHUNKS - 1 - chunk)
        for i in range(br):
            slots = own_slots(dims, chunk, column)
            mask_ref[place, i : i + 1, :] = 2.0 * block_mask(pattern_ref, i, slots, bs, F32)
        for s in range(dims.stride):
            m = chunk * dims.stride + s
            hit = (cell == y_offset_ref[0, m] + step) & (step < y_extent_ref[0, m])
            spread = lax.dot_general(
                y_basis_ref[:, m * bs : (m + 1) * bs],
                hit.astype(F32).astype(BF16),
                (((0,), (0,)), ((), ())),
                preferred_element_type=F32,
            )
            y_ref[place, s * bs : (s + 1) * bs, :] = spread.astype(BF16)
    step = lax.broadcasted_iota(jnp.int32, (EX, tx), 1)
    cell = lax.broadcasted_iota(jnp.int32, (EX, tx), 0)
    for i in range(br):
        hit = (cell == x_offset_ref[i] + step) & (step < x_extent_ref[i])
        spread = jnp.dot(
            hit.astype(F32).astype(BF16),
            x_basis_ref[:, i * bs : (i + 1) * bs],
            preferred_element_type=F32,
        )
        xt_ref[:, i * bs : (i + 1) * bs] = spread.astype(BF16)


def square_kernel(dims, p2_ref, wide_ref, *refs):
    squares_ref, summed_ref = refs[3:5]
    for source, dest in zip(refs[:3], refs[5:]):
        dest[...] = source[...]
    odd = lax.axis_index("row") % 2
    column = lax.axis_index("col")
    bs, br = dims.bs, dims.br
    width = br * bs
    for block in range(CHUNKS):
        place = jnp.where(odd == 1, block, CHUNKS - 1 - block)
        cols = slice(block * width, (block + 1) * width)
        for i in range(br):
            rows = slice(i * bs, (i + 1) * bs)
            squares_ref[place, rows, :] = p2_ref[rows, cols] * wide_ref[i : i + 1, cols].astype(BF16)
    for chunk in range(CHUNKS):
        place = jnp.where(odd == 1, chunk, CHUNKS - 1 - chunk)
        parts = [
            own_block_cols(dims, p2_ref, chunk * dims.stride + s, column)
            for s in range(dims.stride)
        ]
        own = parts[0] if len(parts) == 1 else jnp.concatenate(parts, axis=1)
        summed_ref[place] = 1.5 * own


def paired(terms):
    return [terms[at : at + 2] for at in range(0, len(terms), 2)]


def add_products(square, terms, summed_ref):
    for group in paired(terms):
        tiles = [tile[...] for _, tile in group]
        wide = tiles[0] if len(tiles) == 1 else jnp.concatenate(tiles, axis=1)
        product = jnp.dot(square, wide, preferred_element_type=F32)
        uw = tiles[0].shape[1]
        for at, (place, _) in enumerate(group):
            summed_ref[place] -= product[:, at * uw : (at + 1) * uw]


def first_kernel(squares_ref, before_ref, x1a_ref, x1b_ref, summed_ref):
    summed_ref[...] = before_ref[...]
    own = lambda j: x1a_ref.at[j] if j < NEAR else x1b_ref.at[j - NEAR]
    add_products(
        squares_ref[HD], [(k, own(CHUNKS - 1 - k)) for k in range(CHUNKS)], summed_ref
    )


def stage_kernel(terms, squares_ref, before_ref, *refs):
    summed_ref = refs[-1]
    summed_ref[...] = before_ref[...]
    for distance, pairs in terms:
        add_products(
            squares_ref[HD + distance],
            [(place, refs[which].at[at]) for place, which, at in pairs],
            summed_ref,
        )


def finish(mask_ref, k, total, new_ref, at):
    br, uw = mask_ref.shape[1:]
    bs = total.shape[0] // br
    for i in range(br):
        rows = slice(i * bs, (i + 1) * bs)
        kept = total[rows] * mask_ref[k, i : i + 1, :]
        new_ref[rows, at * uw : (at + 1) * uw] = kept.astype(BF16)


def inner_kernel(
    mask_ref, squares_ref, before_ref, x2p_ref, z3_ref, y_ref, new_ref, half_ref, edges_ref
):
    uw = edges_ref.shape[2]

    def product(distance, *tiles):
        wide = jnp.concatenate(tiles, axis=1)
        return jnp.dot(squares_ref[HD + distance], wide, preferred_element_type=F32)

    low = product(-2, x2p_ref[3], x2p_ref[2])
    mid = product(-2, x2p_ref[1], x2p_ref[0]) + product(3, z3_ref[0], z3_ref[1])
    high = product(3, z3_ref[2], z3_ref[3])
    parts = [low[:, :uw], low[:, uw:], mid[:, :uw], mid[:, uw:], high[:, :uw]]
    for at, part in enumerate(parts):
        finish(mask_ref, at + 1, before_ref[at + 1] - part, new_ref, at)
    edges_ref[0] = before_ref[0]
    edges_ref[1] = before_ref[CHUNKS - 1] - high[:, uw:]
    inner = y_ref[1 : CHUNKS - 1].reshape((CHUNKS - 2) * uw, EY)
    half_ref[...] = jnp.dot(new_ref[...], inner, preferred_element_type=F32)


def last_kernel(
    mask_ref,
    squares_ref,
    edges_ref,
    x2q_ref,
    z1b_ref,
    xt_ref,
    y_ref,
    half_ref,
    new_ref,
    middle_ref,
    rim_a_ref,
    rim_b_ref,
):
    odd = lax.axis_index("row") % 2
    product = lambda d, tile: jnp.dot(squares_ref[HD + d], tile, preferred_element_type=F32)
    finish(mask_ref, 0, edges_ref[0] - product(-2, x2q_ref[0]), new_ref, 0)
    finish(mask_ref, CHUNKS - 1, edges_ref[1] - product(2, z1b_ref[0]), new_ref, 1)
    outer = jnp.concatenate([y_ref[0], y_ref[CHUNKS - 1]], axis=0)
    half = half_ref[...] + jnp.dot(new_ref[...], outer, preferred_element_type=F32)
    extended = jnp.dot(xt_ref[...], half.astype(BF16), preferred_element_type=F32)
    middle_ref[...] = extended[M : M + SX]
    lower, upper = extended[:M], extended[SX + M :]
    rim_a_ref[...] = jnp.where(odd == 1, lower, upper).astype(BF16)
    rim_b_ref[...] = jnp.where(odd == 1, upper, lower).astype(BF16)


def order_kernel(inner_ref, edges_ref, new_ref):
    odd = lax.axis_index("row") % 2
    uw = edges_ref.shape[1] // 2

    @pl.when(odd == 1)
    def _():
        new_ref[:, :uw] = edges_ref[:, :uw]
        new_ref[:, uw : (CHUNKS - 1) * uw] = inner_ref[...]
        new_ref[:, (CHUNKS - 1) * uw :] = edges_ref[:, uw:]

    @pl.when(odd == 0)
    def _():
        new_ref[:, :uw] = edges_ref[:, uw:]
        for at in range(CHUNKS - 2):
            place = CHUNKS - 2 - at
            new_ref[:, place * uw : (place + 1) * uw] = inner_ref[:, at * uw : (at + 1) * uw]
        new_ref[:, (CHUNKS - 1) * uw :] = edges_ref[:, :uw]


def row_rims_kernel(middle_ref, got_a_ref, got_b_ref, center_ref, rim_a_ref, rim_b_ref):
    odd = lax.axis_index("row") % 2
    col_odd = lax.axis_index("col") % 2
    got_a, got_b = got_a_ref[...].astype(F32), got_b_ref[...].astype(F32)
    low = jnp.where(odd == 1, got_a, got_b)
    high = jnp.where(odd == 1, got_b, got_a)
    interior = jnp.concatenate(
        [middle_ref[:M] + low, middle_ref[M : SX - M], middle_ref[SX - M :] + high], axis=0
    )
    center_ref[...] = interior[:, M : M + SY]
    lower = interior[:, :SY].T[:M]
    upper = interior[:, EY - SY :].T[SY - M :]
    rim_a_ref[...] = jnp.where(col_odd == 1, lower, upper).astype(BF16)
    rim_b_ref[...] = jnp.where(col_odd == 1, upper, lower).astype(BF16)


def col_rims_kernel(center_ref, got_a_ref, got_b_ref, grid_ref):
    col_odd = lax.axis_index("col") % 2
    got_a, got_b = got_a_ref[...].astype(F32), got_b_ref[...].astype(F32)
    low = jnp.where(col_odd == 1, got_a, got_b)
    high = jnp.where(col_odd == 1, got_b, got_a)
    none = jnp.zeros((SY - 2 * M, SX), F32)
    grid_ref[...] = center_ref[...] + jnp.concatenate([low, none, high], axis=0).T


def swap_partner(value, axis):
    count = lax.axis_size(axis)
    return lax.ppermute(value, axis, [(s, s ^ 1) for s in range(count)])


def swap_other(value, axis):
    count = lax.axis_size(axis)
    pairs = [(s, (s - 1) % count if s % 2 == 0 else (s + 1) % count) for s in range(count)]
    return lax.ppermute(value, axis, pairs)


def shift_level(value):
    count = lax.axis_size("row")
    pairs = [(s, (s + 2) % count if s % 2 == 0 else (s - 2) % count) for s in range(count)]
    return lax.ppermute(value, "row", pairs)


def after(value, *others):
    return lax.optimization_barrier((value,) + others)[0]


def call(kernel, outs, ins, scratch=(), beside=0, stay=(), outs_stay=False, limit=24):
    shapes = [jax.ShapeDtypeStruct(shape, dtype) for shape, dtype in outs]
    specs = [
        HBM
        if at in stay
        else SMEM
        if jnp.issubdtype(value.dtype, jnp.integer)
        else VMEM
        for at, value in enumerate(ins)
    ]
    moved = sum(value.size * value.dtype.itemsize for value in list(ins) + shapes)
    return pl.pallas_call(
        kernel,
        out_shape=shapes,
        in_specs=specs,
        out_specs=[HBM if outs_stay else VMEM] * len(shapes),
        scratch_shapes=list(scratch),
        compiler_params=pltpu.CompilerParams(vmem_limit_bytes=limit * 2**20),
        cost_estimate=pl.CostEstimate(
            flops=beside * 10**9, bytes_accessed=moved, transcendentals=0
        ),
    )(*ins)


def shards(p2_panel, density, pattern, x_basis, x_offset, x_extent, y_basis, y_offset, y_extent):
    dims = Dims(pattern, x_basis, lax.axis_size("col"))
    rows, uw = dims.rows, dims.uw
    chunks = lambda count: ((count, rows, uw), BF16)
    total = ((CHUNKS, rows, uw), F32)

    parts = CHUNKS if uw % 128 == 0 else 1
    own_p, own_q, own_z, own_zb = call(
        functools.partial(mask_kernel, dims),
        [chunks(NEAR), chunks(CHUNKS - NEAR), chunks(NEAR), chunks(AHEAD - NEAR)],
        [pattern, density],
        scratch=[
            pltpu.SMEM(pattern.shape, jnp.int32),
            pltpu.VMEM((parts, rows, CHUNKS * uw // parts), BF16),
            pltpu.VMEM((CHUNKS, rows, uw), BF16),
            pltpu.SemaphoreType.DMA(()),
            pltpu.SemaphoreType.DMA((parts,)),
            pltpu.SemaphoreType.DMA((NEAR,)),
            pltpu.SemaphoreType.DMA((CHUNKS - NEAR,)),
            pltpu.SemaphoreType.DMA((AHEAD,)),
        ],
        stay=(0, 1),
        outs_stay=True,
        limit=60,
    )
    x1p = swap_partner(own_p, "row")
    z1 = shift_level(own_z)
    x1q = swap_partner(own_q, "row")

    small = [pattern, x_offset, x_extent, y_offset, y_extent, x_basis.T, y_basis[0].T]
    xt, y_spread, mask, wide = call(
        functools.partial(spread_kernel, dims),
        [
            ((EX, rows), BF16),
            ((CHUNKS, uw, EY), BF16),
            ((CHUNKS, dims.br, uw), F32),
            ((dims.br, dims.win * dims.bs), F32),
        ],
        small,
        scratch=[
            (pltpu.SMEM if jnp.issubdtype(value.dtype, jnp.integer) else pltpu.VMEM)(
                value.shape, value.dtype
            )
            for value in small
        ]
        + [pltpu.SemaphoreType.DMA((len(small),))],
        stay=range(len(small)),
        limit=60,
        beside=6,
    )
    kept = [xt, y_spread, mask]
    squares, summed, xt, y_spread, mask = call(
        functools.partial(square_kernel, dims),
        [((CHUNKS, rows, rows), BF16), total] + [(value.shape, value.dtype) for value in kept],
        [p2_panel, wide] + kept,
        beside=1,
    )
    ready = summed

    def stage(summed, terms, beside=0):
        tiles = []
        for _, pairs in terms:
            for _, tile, _ in pairs:
                if not any(tile is known for known in tiles):
                    tiles.append(tile)
        spot = lambda tile: next(at for at, known in enumerate(tiles) if known is tile)
        listed = [(d, [(place, spot(tile), at) for place, tile, at in pairs]) for d, pairs in terms]
        return call(
            functools.partial(stage_kernel, listed),
            [total],
            [squares, summed] + tiles,
            beside=beside,
        )[0]

    (summed,) = call(first_kernel, [total], [squares, summed, own_p, own_q])
    z2p = shift_level(after(x1p, ready))
    x3 = swap_partner(z1, "row")
    z2q = shift_level(x1q[: 2 * HD - NEAR])
    z1b = shift_level(after(own_zb, z2p))
    partner = [(j - 1, x1p, j) for j in range(1, NEAR)]
    partner += [(j - 1, x1q, j - NEAR) for j in range(NEAR, CHUNKS)]
    summed = stage(
        summed, [(-1, partner), (2, [(j + 2, z1, j) for j in range(NEAR)])], beside=3
    )
    x2p = swap_partner(after(z2p, summed), "row")
    z3 = shift_level(z2p)
    summed = stage(summed, [(1, [(j + 1, z2p, j) for j in range(NEAR)])])
    x2q = swap_partner(z2q[: AHEAD - NEAR], "row")
    summed = stage(
        summed,
        [
            (1, [(j + 1, z2q, j - NEAR) for j in range(NEAR, 2 * HD)]),
            (-3, [(3 - j, x3, j) for j in range(NEAR)]),
        ],
        beside=4,
    )
    new_inner, half, edges = call(
        inner_kernel,
        [((rows, (CHUNKS - 2) * uw), BF16), ((rows, EY), F32), ((2, rows, uw), F32)],
        [mask, squares, summed, x2p, z3, y_spread],
        beside=0,
    )
    new_edges, middle, rim_a, rim_b = call(
        last_kernel,
        [((rows, 2 * uw), BF16), ((SX, EY), F32), ((M, EY), BF16), ((M, EY), BF16)],
        [mask, squares, edges, x2q, z1b, xt, y_spread, half],
    )
    (new_density,) = call(
        order_kernel, [((rows, dims.wc * dims.bs), BF16)], [new_inner, new_edges]
    )
    got_a = swap_partner(rim_a, "row")
    got_b = swap_other(rim_b, "row")
    center, rim_a, rim_b = call(
        row_rims_kernel,
        [((SX, SY), F32), ((M, SX), BF16), ((M, SX), BF16)],
        [after(middle, new_density), got_a, got_b],
    )
    got_a = swap_partner(rim_a, "col")
    got_b = swap_other(rim_b, "col")
    (grid_density,) = call(col_rims_kernel, [((SX, SY), F32)], [center, got_a, got_b])
    return new_density, grid_density


def solution(mesh):
    placed = (
        P("row", None),
        P("row", "col"),
        P("row", None),
        P("row", None),
        P("row"),
        P("row"),
        P("row", "col", None),
        P("row", "col"),
        P("row", "col"),
    )
    return jax.shard_map(
        shards,
        mesh=mesh,
        in_specs=placed,
        out_specs=(P("row", "col"), P("row", "col")),
        check_vma=False,
    )
```

```python
import functools

import jax
import jax.numpy as jnp
from jax import lax
from jax.experimental import pallas as pl
from jax.experimental.pallas import tpu as pltpu
from jax.sharding import PartitionSpec as P

HD = 3
SX = 128
SY = 128
M = 32
EX = SX + 2 * M
EY = SY + 2 * M
CHUNKS = 2 * HD + 1
NEAR = HD + 1
AHEAD = HD + 2
VMEM = pl.BlockSpec(memory_space=pltpu.VMEM)
SMEM = pl.BlockSpec(memory_space=pltpu.SMEM)
HBM = pl.BlockSpec(memory_space=pltpu.HBM)
F32 = jnp.float32
BF16 = jnp.bfloat16


class Dims:
    def __init__(self, pattern, x_basis, n_col):
        self.br, self.win = pattern.shape
        self.bs = x_basis.shape[0] // self.br
        self.n_col = n_col
        self.wc = self.win // n_col
        self.stride = self.br // n_col
        self.uw = self.stride * self.bs
        self.rows = self.br * self.bs


def block_mask(pattern_ref, block_row, slots, bs, dtype):
    lane = lax.broadcasted_iota(jnp.int32, (1, bs * len(slots)), 1)
    row = jnp.zeros((1, bs * len(slots)), jnp.int32)
    for place, slot in enumerate(slots):
        inside = (lane >= place * bs) & (lane < (place + 1) * bs)
        row = jnp.where(inside, pattern_ref[block_row, slot], row)
    return row.astype(F32).astype(dtype)


def own_slots(dims, chunk, column):
    return [dims.n_col * (chunk * dims.stride + s) + column for s in range(dims.stride)]


def mask_kernel(
    dims,
    pattern_hbm,
    density_hbm,
    x1a_ref,
    x1b_ref,
    *refs,
):
    z1_refs, refs = refs[:-8], refs[-8:]
    pattern_ref, tile_ref, kept_ref, pattern_sem, tile_sems, x1a_sem, x1b_sem, z1_sem = refs
    odd = lax.axis_index("row") % 2
    column = lax.axis_index("col")
    bs, uw = dims.bs, dims.uw
    wide = tile_ref.shape[2]
    fetch_pattern = pltpu.make_async_copy(pattern_hbm, pattern_ref, pattern_sem)
    fetch_pattern.start()
    fetches = []
    for part in range(tile_ref.shape[0]):
        cols = pl.ds(part * wide, wide)
        fetch = pltpu.make_async_copy(density_hbm.at[:, cols], tile_ref.at[part], tile_sems.at[part])
        fetch.start()
        fetches.append(fetch)
    fetch_pattern.wait()
    near, first = x1a_ref.shape[0], z1_refs[0].shape[0]

    def copies_of(chunk, lane_odd):
        own = chunk if lane_odd else CHUNKS - 1 - chunk
        sent = CHUNKS - 1 - own
        tile = kept_ref.at[chunk]
        found = [
            pltpu.make_async_copy(tile, x1a_ref.at[sent], x1a_sem.at[sent])
            if sent < near
            else pltpu.make_async_copy(tile, x1b_ref.at[sent - near], x1b_sem.at[sent - near])
        ]
        if own < 5:
            dest = z1_refs[0].at[own] if own < first else z1_refs[1].at[own - first]
            found.append(pltpu.make_async_copy(tile, dest, z1_sem.at[own]))
        return found

    arrived = 0
    for chunk in range(CHUNKS):
        part, start = divmod(chunk * uw, wide)
        if part == arrived:
            fetches[part].wait()
            arrived += 1
        for i in range(dims.br):
            rows = slice(i * bs, (i + 1) * bs)
            mask = block_mask(pattern_ref, i, own_slots(dims, chunk, column), bs, BF16)
            kept_ref[chunk, rows, :] = tile_ref[part, rows, start : start + uw] * mask
        for lane_odd in (0, 1):

            @pl.when(odd == lane_odd)
            def _():
                for copy in copies_of(chunk, lane_odd):
                    copy.start()

    for lane_odd in (0, 1):

        @pl.when(odd == lane_odd)
        def _():
            for chunk in range(CHUNKS):
                for copy in copies_of(chunk, lane_odd):
                    copy.wait()


def own_block_cols(dims, p2_ref, slot, column):
    pair = pl.multiple_of((dims.n_col * slot // 2 + column // 2) * 2 * dims.bs, 2 * dims.bs)
    wide = p2_ref[:, pl.ds(pair, 2 * dims.bs)].astype(F32)
    return jnp.where(column % 2 == 1, wide[:, dims.bs :], wide[:, : dims.bs])


def spread_kernel(dims, *refs):
    inputs, refs = refs[:7], refs[7:]
    xt_ref, y_ref, mask_ref, wide_ref = refs[:4]
    held, sems = refs[4:11], refs[11]
    copies = [
        pltpu.make_async_copy(source, dest, sems.at[at])
        for at, (source, dest) in enumerate(zip(inputs, held))
    ]
    for copy in copies:
        copy.start()
    for copy in copies:
        copy.wait()
    pattern_ref, x_offset_ref, x_extent_ref, y_offset_ref, y_extent_ref, x_basis_ref, y_basis_ref = held
    odd = lax.axis_index("row") % 2
    column = lax.axis_index("col")
    bs, br = dims.bs, dims.br
    width = br * bs
    for i in range(br):
        for block in range(CHUNKS):
            slots = [block * br + t for t in range(br)]
            mask = block_mask(pattern_ref, i, slots, bs, F32)
            wide_ref[i : i + 1, block * width : (block + 1) * width] = mask
    tx = y_basis_ref.shape[0]
    step = lax.broadcasted_iota(jnp.int32, (tx, EY), 0)
    cell = lax.broadcasted_iota(jnp.int32, (tx, EY), 1)
    for chunk in range(CHUNKS):
        place = jnp.where(odd == 1, chunk, CHUNKS - 1 - chunk)
        for i in range(br):
            slots = own_slots(dims, chunk, column)
            mask_ref[place, i : i + 1, :] = 2.0 * block_mask(pattern_ref, i, slots, bs, F32)
        for s in range(dims.stride):
            m = chunk * dims.stride + s
            hit = (cell == y_offset_ref[0, m] + step) & (step < y_extent_ref[0, m])
            spread = lax.dot_general(
                y_basis_ref[:, m * bs : (m + 1) * bs],
                hit.astype(F32).astype(BF16),
                (((0,), (0,)), ((), ())),
                preferred_element_type=F32,
            )
            y_ref[place, s * bs : (s + 1) * bs, :] = spread.astype(BF16)
    step = lax.broadcasted_iota(jnp.int32, (EX, tx), 1)
    cell = lax.broadcasted_iota(jnp.int32, (EX, tx), 0)
    for i in range(br):
        hit = (cell == x_offset_ref[i] + step) & (step < x_extent_ref[i])
        spread = jnp.dot(
            hit.astype(F32).astype(BF16),
            x_basis_ref[:, i * bs : (i + 1) * bs],
            preferred_element_type=F32,
        )
        xt_ref[:, i * bs : (i + 1) * bs] = spread.astype(BF16)


def square_kernel(dims, p2_ref, wide_ref, *refs):
    squares_ref, summed_ref = refs[3:5]
    for source, dest in zip(refs[:3], refs[5:]):
        dest[...] = source[...]
    odd = lax.axis_index("row") % 2
    column = lax.axis_index("col")
    bs, br = dims.bs, dims.br
    width = br * bs
    for block in range(CHUNKS):
        place = jnp.where(odd == 1, block, CHUNKS - 1 - block)
        cols = slice(block * width, (block + 1) * width)
        for i in range(br):
            rows = slice(i * bs, (i + 1) * bs)
            squares_ref[place, rows, :] = p2_ref[rows, cols] * wide_ref[i : i + 1, cols].astype(BF16)
    for chunk in range(CHUNKS):
        place = jnp.where(odd == 1, chunk, CHUNKS - 1 - chunk)
        parts = [
            own_block_cols(dims, p2_ref, chunk * dims.stride + s, column)
            for s in range(dims.stride)
        ]
        own = parts[0] if len(parts) == 1 else jnp.concatenate(parts, axis=1)
        summed_ref[place] = 1.5 * own


def paired(terms):
    return [terms[at : at + 2] for at in range(0, len(terms), 2)]


def add_products(square, terms, summed_ref):
    for group in paired(terms):
        tiles = [tile[...] for _, tile in group]
        wide = tiles[0] if len(tiles) == 1 else jnp.concatenate(tiles, axis=1)
        product = jnp.dot(square, wide, preferred_element_type=F32)
        uw = tiles[0].shape[1]
        for at, (place, _) in enumerate(group):
            summed_ref[place] -= product[:, at * uw : (at + 1) * uw]


def first_kernel(squares_ref, before_ref, x1a_ref, x1b_ref, summed_ref):
    summed_ref[...] = before_ref[...]
    own = lambda j: x1a_ref.at[j] if j < NEAR else x1b_ref.at[j - NEAR]
    add_products(
        squares_ref[HD], [(k, own(CHUNKS - 1 - k)) for k in range(CHUNKS)], summed_ref
    )


def stage_kernel(terms, squares_ref, before_ref, *refs):
    summed_ref = refs[-1]
    summed_ref[...] = before_ref[...]
    for distance, pairs in terms:
        add_products(
            squares_ref[HD + distance],
            [(place, refs[which].at[at]) for place, which, at in pairs],
            summed_ref,
        )


def finish(mask_ref, k, total, new_ref, at):
    br, uw = mask_ref.shape[1:]
    bs = total.shape[0] // br
    for i in range(br):
        rows = slice(i * bs, (i + 1) * bs)
        kept = total[rows] * mask_ref[k, i : i + 1, :]
        new_ref[rows, at * uw : (at + 1) * uw] = kept.astype(BF16)


def inner_kernel(
    mask_ref, squares_ref, before_ref, x2p_ref, z3_ref, y_ref, new_ref, half_ref, edges_ref
):
    uw = edges_ref.shape[2]

    def product(distance, *tiles):
        wide = jnp.concatenate(tiles, axis=1)
        return jnp.dot(squares_ref[HD + distance], wide, preferred_element_type=F32)

    low = product(-2, x2p_ref[3], x2p_ref[2])
    mid = product(-2, x2p_ref[1], x2p_ref[0]) + product(3, z3_ref[0], z3_ref[1])
    high = product(3, z3_ref[2], z3_ref[3])
    parts = [low[:, :uw], low[:, uw:], mid[:, :uw], mid[:, uw:], high[:, :uw]]
    for at, part in enumerate(parts):
        finish(mask_ref, at + 1, before_ref[at + 1] - part, new_ref, at)
    edges_ref[0] = before_ref[0]
    edges_ref[1] = before_ref[CHUNKS - 1] - high[:, uw:]
    inner = y_ref[1 : CHUNKS - 1].reshape((CHUNKS - 2) * uw, EY)
    half_ref[...] = jnp.dot(new_ref[...], inner, preferred_element_type=F32)


def last_kernel(
    mask_ref,
    squares_ref,
    edges_ref,
    x2q_ref,
    z1b_ref,
    xt_ref,
    y_ref,
    half_ref,
    new_ref,
    middle_ref,
    rim_a_ref,
    rim_b_ref,
):
    odd = lax.axis_index("row") % 2
    product = lambda d, tile: jnp.dot(squares_ref[HD + d], tile, preferred_element_type=F32)
    finish(mask_ref, 0, edges_ref[0] - product(-2, x2q_ref[0]), new_ref, 0)
    finish(mask_ref, CHUNKS - 1, edges_ref[1] - product(2, z1b_ref[0]), new_ref, 1)
    outer = jnp.concatenate([y_ref[0], y_ref[CHUNKS - 1]], axis=0)
    half = half_ref[...] + jnp.dot(new_ref[...], outer, preferred_element_type=F32)
    extended = jnp.dot(xt_ref[...], half.astype(BF16), preferred_element_type=F32)
    middle_ref[...] = extended[M : M + SX]
    lower, upper = extended[:M], extended[SX + M :]
    rim_a_ref[...] = jnp.where(odd == 1, lower, upper).astype(BF16)
    rim_b_ref[...] = jnp.where(odd == 1, upper, lower).astype(BF16)


def order_kernel(inner_ref, edges_ref, new_ref):
    odd = lax.axis_index("row") % 2
    uw = edges_ref.shape[1] // 2

    @pl.when(odd == 1)
    def _():
        new_ref[:, :uw] = edges_ref[:, :uw]
        new_ref[:, uw : (CHUNKS - 1) * uw] = inner_ref[...]
        new_ref[:, (CHUNKS - 1) * uw :] = edges_ref[:, uw:]

    @pl.when(odd == 0)
    def _():
        new_ref[:, :uw] = edges_ref[:, uw:]
        for at in range(CHUNKS - 2):
            place = CHUNKS - 2 - at
            new_ref[:, place * uw : (place + 1) * uw] = inner_ref[:, at * uw : (at + 1) * uw]
        new_ref[:, (CHUNKS - 1) * uw :] = edges_ref[:, :uw]


def row_rims_kernel(middle_ref, got_a_ref, got_b_ref, center_ref, rim_a_ref, rim_b_ref):
    odd = lax.axis_index("row") % 2
    col_odd = lax.axis_index("col") % 2
    got_a, got_b = got_a_ref[...].astype(F32), got_b_ref[...].astype(F32)
    low = jnp.where(odd == 1, got_a, got_b)
    high = jnp.where(odd == 1, got_b, got_a)
    interior = jnp.concatenate(
        [middle_ref[:M] + low, middle_ref[M : SX - M], middle_ref[SX - M :] + high], axis=0
    )
    center_ref[...] = interior[:, M : M + SY]
    lower = interior[:, :SY].T[:M]
    upper = interior[:, EY - SY :].T[SY - M :]
    rim_a_ref[...] = jnp.where(col_odd == 1, lower, upper).astype(BF16)
    rim_b_ref[...] = jnp.where(col_odd == 1, upper, lower).astype(BF16)


def col_rims_kernel(center_ref, got_a_ref, got_b_ref, grid_ref):
    col_odd = lax.axis_index("col") % 2
    got_a, got_b = got_a_ref[...].astype(F32), got_b_ref[...].astype(F32)
    low = jnp.where(col_odd == 1, got_a, got_b)
    high = jnp.where(col_odd == 1, got_b, got_a)
    none = jnp.zeros((SY - 2 * M, SX), F32)
    grid_ref[...] = center_ref[...] + jnp.concatenate([low, none, high], axis=0).T


def swap_partner(value, axis):
    count = lax.axis_size(axis)
    return lax.ppermute(value, axis, [(s, s ^ 1) for s in range(count)])


def swap_other(value, axis):
    count = lax.axis_size(axis)
    pairs = [(s, (s - 1) % count if s % 2 == 0 else (s + 1) % count) for s in range(count)]
    return lax.ppermute(value, axis, pairs)


def shift_level(value):
    count = lax.axis_size("row")
    pairs = [(s, (s + 2) % count if s % 2 == 0 else (s - 2) % count) for s in range(count)]
    return lax.ppermute(value, "row", pairs)


def after(value, *others):
    return lax.optimization_barrier((value,) + others)[0]


def call(kernel, outs, ins, scratch=(), beside=0, stay=(), outs_stay=False, limit=24):
    shapes = [jax.ShapeDtypeStruct(shape, dtype) for shape, dtype in outs]
    specs = [
        HBM
        if at in stay
        else SMEM
        if jnp.issubdtype(value.dtype, jnp.integer)
        else VMEM
        for at, value in enumerate(ins)
    ]
    moved = sum(value.size * value.dtype.itemsize for value in list(ins) + shapes)
    return pl.pallas_call(
        kernel,
        out_shape=shapes,
        in_specs=specs,
        out_specs=[HBM if outs_stay else VMEM] * len(shapes),
        scratch_shapes=list(scratch),
        compiler_params=pltpu.CompilerParams(vmem_limit_bytes=limit * 2**20),
        cost_estimate=pl.CostEstimate(
            flops=beside * 10**9, bytes_accessed=moved, transcendentals=0
        ),
    )(*ins)


def shards(p2_panel, density, pattern, x_basis, x_offset, x_extent, y_basis, y_offset, y_extent):
    dims = Dims(pattern, x_basis, lax.axis_size("col"))
    rows, uw = dims.rows, dims.uw
    chunks = lambda count: ((count, rows, uw), BF16)
    total = ((CHUNKS, rows, uw), F32)

    parts = CHUNKS if uw % 128 == 0 else 1
    own_p, own_q, own_z, own_zb = call(
        functools.partial(mask_kernel, dims),
        [chunks(NEAR), chunks(CHUNKS - NEAR), chunks(NEAR), chunks(AHEAD - NEAR)],
        [pattern, density],
        scratch=[
            pltpu.SMEM(pattern.shape, jnp.int32),
            pltpu.VMEM((parts, rows, CHUNKS * uw // parts), BF16),
            pltpu.VMEM((CHUNKS, rows, uw), BF16),
            pltpu.SemaphoreType.DMA(()),
            pltpu.SemaphoreType.DMA((parts,)),
            pltpu.SemaphoreType.DMA((NEAR,)),
            pltpu.SemaphoreType.DMA((CHUNKS - NEAR,)),
            pltpu.SemaphoreType.DMA((AHEAD,)),
        ],
        stay=(0, 1),
        outs_stay=True,
        limit=60,
    )
    x1p = swap_partner(own_p, "row")
    z1 = shift_level(own_z)
    x1q = swap_partner(own_q, "row")

    small = [pattern, x_offset, x_extent, y_offset, y_extent, x_basis.T, y_basis[0].T]
    xt, y_spread, mask, wide = call(
        functools.partial(spread_kernel, dims),
        [
            ((EX, rows), BF16),
            ((CHUNKS, uw, EY), BF16),
            ((CHUNKS, dims.br, uw), F32),
            ((dims.br, dims.win * dims.bs), F32),
        ],
        small,
        scratch=[
            (pltpu.SMEM if jnp.issubdtype(value.dtype, jnp.integer) else pltpu.VMEM)(
                value.shape, value.dtype
            )
            for value in small
        ]
        + [pltpu.SemaphoreType.DMA((len(small),))],
        stay=range(len(small)),
        limit=60,
        beside=6,
    )
    kept = [xt, y_spread, mask]
    squares, summed, xt, y_spread, mask = call(
        functools.partial(square_kernel, dims),
        [((CHUNKS, rows, rows), BF16), total] + [(value.shape, value.dtype) for value in kept],
        [p2_panel, wide] + kept,
        beside=1,
    )
    ready = summed

    def stage(summed, terms, beside=0):
        tiles = []
        for _, pairs in terms:
            for _, tile, _ in pairs:
                if not any(tile is known for known in tiles):
                    tiles.append(tile)
        spot = lambda tile: next(at for at, known in enumerate(tiles) if known is tile)
        listed = [(d, [(place, spot(tile), at) for place, tile, at in pairs]) for d, pairs in terms]
        return call(
            functools.partial(stage_kernel, listed),
            [total],
            [squares, summed] + tiles,
            beside=beside,
        )[0]

    (summed,) = call(first_kernel, [total], [squares, summed, own_p, own_q])
    z2p = shift_level(after(x1p, ready))
    x3 = swap_partner(z1, "row")
    z2q = shift_level(x1q[: 2 * HD - NEAR])
    z1b = shift_level(after(own_zb, z2p))
    partner = [(j - 1, x1p, j) for j in range(1, NEAR)]
    partner += [(j - 1, x1q, j - NEAR) for j in range(NEAR, CHUNKS)]
    summed = stage(
        summed, [(-1, partner), (2, [(j + 2, z1, j) for j in range(NEAR)])], beside=3
    )
    x2p = swap_partner(after(z2p, summed), "row")
    z3 = shift_level(z2p)
    summed = stage(summed, [(1, [(j + 1, z2p, j) for j in range(NEAR)])])
    x2q = swap_partner(z2q[: AHEAD - NEAR], "row")
    summed = stage(
        summed,
        [
            (1, [(j + 1, z2q, j - NEAR) for j in range(NEAR, 2 * HD)]),
            (-3, [(3 - j, x3, j) for j in range(NEAR)]),
        ],
        beside=4,
    )
    new_inner, half, edges = call(
        inner_kernel,
        [((rows, (CHUNKS - 2) * uw), BF16), ((rows, EY), F32), ((2, rows, uw), F32)],
        [mask, squares, summed, x2p, z3, y_spread],
        beside=0,
    )
    new_edges, middle, rim_a, rim_b = call(
        last_kernel,
        [((rows, 2 * uw), BF16), ((SX, EY), F32), ((M, EY), BF16), ((M, EY), BF16)],
        [mask, squares, edges, x2q, z1b, xt, y_spread, half],
    )
    (new_density,) = call(
        order_kernel, [((rows, dims.wc * dims.bs), BF16)], [new_inner, new_edges]
    )
    got_a = swap_partner(rim_a, "row")
    got_b = swap_other(rim_b, "row")
    center, rim_a, rim_b = call(
        row_rims_kernel,
        [((SX, SY), F32), ((M, SX), BF16), ((M, SX), BF16)],
        [middle, got_a, got_b],
    )
    got_a = swap_partner(rim_a, "col")
    got_b = swap_other(rim_b, "col")
    (grid_density,) = call(col_rims_kernel, [((SX, SY), F32)], [center, got_a, got_b])
    return new_density, grid_density


def solution(mesh):
    placed = (
        P("row", None),
        P("row", "col"),
        P("row", None),
        P("row", None),
        P("row"),
        P("row"),
        P("row", "col", None),
        P("row", "col"),
        P("row", "col"),
    )
    return jax.shard_map(
        shards,
        mesh=mesh,
        in_specs=placed,
        out_specs=(P("row", "col"), P("row", "col")),
        check_vma=False,
    )
```
